32 devices in a mesh: seq: 4 (over y, x), fsdp: 8 (over z, core).
Axes of the slice: x: 2, y: 2, z: 4, core: 2. Of those that a mesh axis runs over, the one named last changes fastest.
Arguments:
- inputs: bfloat16 [4096, 2048], P(('fsdp', 'seq')), may hold values from -6 to 6
- positions: int32 [4096], P(('fsdp', 'seq')), may hold values from 0 to 766, as said below
- seq_ids: int32 [4096], P(('fsdp', 'seq')), may hold values from 0 to 15, as said below
- attn_gain: bfloat16 [2048], P(('fsdp', 'seq')), may hold values from 0.5 to 1.5
- w_query: bfloat16 [2048, 2048], P(('fsdp', 'seq')), may hold values from -0.125 to 0.125
- w_key: bfloat16 [2048, 2048], P(('fsdp', 'seq')), may hold values from -0.125 to 0.125
- w_value: bfloat16 [2048, 2048], P(('fsdp', 'seq')), may hold values from -0.125 to 0.125
- w_out: bfloat16 [2048, 2048], P(('fsdp', 'seq')), may hold values from -1 to 1
- ffn_gain: bfloat16 [2048], P(('fsdp', 'seq')), may hold values from 0.5 to 1.5
- w_gate: bfloat16 [2048, 8192], P(('fsdp', 'seq')), may hold values from -0.125 to 0.125
- w_up: bfloat16 [2048, 8192], P(('fsdp', 'seq')), may hold values from -0.125 to 0.125
- w_down: bfloat16 [8192, 2048], P(('fsdp', 'seq')), may hold values from -0.0625 to 0.0625
- cotangent: bfloat16 [4096, 2048], P(('fsdp', 'seq')), may hold values from -6 to 6
Outputs:
- layer_out: bfloat16 [4096, 2048], P(('fsdp', 'seq'))
- grad_input: float32 [4096, 2048], P(('fsdp', 'seq'))
- grad_attn_gain: float32 [2048], P(('fsdp', 'seq'))
- grad_query: float32 [2048, 2048], P(('fsdp', 'seq'))
- grad_key: float32 [2048, 2048], P(('fsdp', 'seq'))
- grad_value: float32 [2048, 2048], P(('fsdp', 'seq'))
- grad_out: float32 [2048, 2048], P(('fsdp', 'seq'))
- grad_ffn_gain: float32 [2048], P(('fsdp', 'seq'))
- grad_gate: float32 [2048, 8192], P(('fsdp', 'seq'))
- grad_up: float32 [2048, 8192], P(('fsdp', 'seq'))
- grad_down: float32 [8192, 2048], P(('fsdp', 'seq'))
The draws below stay inside these ranges and needn't reach their ends.
Inputs may be any that keep to these rules, and one draw needn't show every extreme that they name: `seq_ids`: rows g * 512 to (g + 1) * 512 - 1 hold two documents, ids 2 g and 2 g + 1 in this order; the first holds 128 to 384 rows, exactly 384 in the first packed sequence. Within each document positions start at 0 at its first row and rise by 1 or 2 from one row to the next; in the first packed sequence they rise by 2 at every row.
All inputs are finite; a program needn't handle non-finite values.
Results may differ from the reference program's by a relative error of at most 0.014.
Values may be sent and summed in bfloat16 or wider, within the bound.
No kernel may reach another device: no remote copies, remote signals or barrier semaphores. Data moves between devices by JAX's collectives and lax.ppermute only.
A program may use at most 704 MiB of HBM per device.

```python
import math
import jax
import jax.numpy as jnp
from jax import lax

D = 2048
HEADS = 16
HEAD_DIM = 128
FF = 8192
GROUP_TOK = 512
TOKENS = 4096


def doc_layout(key):
    group_count = TOKENS // GROUP_TOK
    bounds = jax.random.randint(jax.random.fold_in(key, 7), (group_count, 1), GROUP_TOK // 4, 3 * GROUP_TOK // 4 + 1)
    first_group = (jnp.arange(group_count, dtype=jnp.int32) == 0)[:, None]
    bounds = jnp.where(first_group, 3 * GROUP_TOK // 4, bounds).astype(jnp.int32)
    row_index = jnp.arange(GROUP_TOK, dtype=jnp.int32)[None, :]
    second = (row_index >= bounds).astype(jnp.int32)
    strides = jax.random.randint(jax.random.fold_in(key, 8), (group_count, GROUP_TOK), 1, 3)
    strides = jnp.where(first_group, 2, strides).astype(jnp.int32)
    climbed = jnp.cumsum(strides, axis=1)
    doc_base = jnp.where(second == 1, jnp.take_along_axis(climbed, bounds, axis=1), climbed[:, :1])
    places = (climbed - doc_base).reshape(-1).astype(jnp.int32)
    doc_ids = (2 * jnp.arange(group_count, dtype=jnp.int32)[:, None] + second).reshape(-1).astype(jnp.int32)
    return (places, doc_ids)


def draw_positions(key, part):
    return doc_layout(key)[0]


def draw_seq_ids(key, part):
    return doc_layout(key)[1]


def strengthened(drawn, own_key, source, target, parts, factor):
    def block_of(position):
        return (jnp.arange(drawn.shape[position]) // (drawn.shape[position] // parts)).reshape((-1,) + (1,) * (drawn.ndim - 1 - position))

    one_side = jax.random.permutation(own_key, parts)[block_of(target)]
    other_side = (block_of(target) + parts // 2) % parts
    return jnp.where((block_of(source) == one_side) | (block_of(source) == other_side), factor * drawn, drawn)


def levels(stream_key, extent, cuts, smallest, high):
    def one(axis_at, shards_of):
        steps = jax.random.uniform(jax.random.fold_in(jax.random.fold_in(stream_key, 6), axis_at), (shards_of,), jnp.float32, smallest / len(cuts), high / len(cuts))
        return jnp.repeat(jnp.exp(steps), extent[axis_at] // shards_of).reshape((-1,) + (1,) * (len(extent) - axis_at - 1))

    loudness = one(*cuts[0])
    for cut in cuts[1:]:
        loudness = loudness * one(*cut)
    return loudness


def scatter_about(own_key, dims, spread, bound, cuts=(), kind=jnp.bfloat16):
    values = jax.random.normal(own_key, dims, jnp.float32) * spread
    if len(cuts) > 0:
        values = levels(own_key, dims, cuts, -0.22, 0.18) * values
    return jnp.clip(values, min=-bound, max=bound).astype(kind)


def gaussian_with(key, extent, spread, limit, shards, heavy, kind=jnp.bfloat16):
    array = spread * jax.random.normal(key, extent, jnp.float32)
    if shards:
        array = array * levels(key, extent, shards, -0.22, 0.18)
    return jnp.clip(strengthened(array, jax.random.fold_in(key, 3), *heavy), -limit, limit).astype(kind)


def setup_inputs(seed: int = 0) -> dict:
    arg_keys = jax.random.split(jax.random.key(seed), 14)
    inputs = gaussian_with(arg_keys[0], (TOKENS, D), 1.0, 6.0, ((0, 32),), (0, 1, 32, 2.75))
    positions = draw_positions(jax.random.fold_in(arg_keys[13], 71), 0)
    seq_ids = draw_seq_ids(jax.random.fold_in(arg_keys[13], 71), 0)
    attn_gain = jnp.clip(1.0 + 0.1 * jax.random.normal(arg_keys[3], (D,), jnp.float32), 0.5, 1.5).astype(jnp.bfloat16)
    w_query = scatter_about(arg_keys[4], (D, D), D ** -0.5, 0.125, ((0, 32),))
    w_key = scatter_about(arg_keys[5], (D, D), D ** -0.5, 0.125, ((0, 32),))
    w_value = scatter_about(arg_keys[6], (D, D), D ** -0.5, 0.125, ((0, 32),))
    w_out = scatter_about(arg_keys[7], (D, D), (max(1, 8 * D // GROUP_TOK)) ** -0.5, 1.0, ((0, 32),))
    ffn_gain = jnp.clip(1.0 + 0.1 * jax.random.normal(arg_keys[8], (D,), jnp.float32), 0.5, 1.5).astype(jnp.bfloat16)
    w_gate = scatter_about(arg_keys[9], (D, FF), D ** -0.5, 0.125, ((0, 32),))
    w_up = scatter_about(arg_keys[10], (D, FF), D ** -0.5, 0.125, ((0, 32),))
    w_down = scatter_about(arg_keys[11], (FF, D), FF ** -0.5, 0.0625, ((0, 32),))
    cotangent = scatter_about(arg_keys[12], (TOKENS, D), 1.0, 6.0, ((0, 32),))
    return {"inputs": inputs, "positions": positions, "seq_ids": seq_ids, "attn_gain": attn_gain, "w_query": w_query, "w_key": w_key, "w_value": w_value, "w_out": w_out, "ffn_gain": ffn_gain, "w_gate": w_gate, "w_up": w_up, "w_down": w_down, "cotangent": cotangent}


EPSILON = 1e-05

@jax.custom_vjp
def low(v):
    return lax.optimization_barrier(v.astype(jnp.bfloat16)).astype(jnp.float32)

@jax.custom_vjp
def low_back(v):
    return v

def low_keep(v):
    return (low(v), None)

def low_pass(kept, grad):
    return (grad,)

def back_keep(v):
    return (v, None)

def back_low(kept, grad):
    return (low(grad),)
low.defvjp(low_keep, low_pass)
low_back.defvjp(back_keep, back_low)

def rope_tables(positions, head_dim):
    half_dim = head_dim // 2
    frequency = 10000.0 ** (-(jnp.arange(half_dim, dtype=jnp.float32) * 2.0) / head_dim)
    angles = positions.astype(jnp.float32)[:, None] * frequency[None, :]
    return (jnp.cos(angles)[:, None, :], jnp.sin(angles)[:, None, :])

def rotate(field, cosine_table, sine_table):
    half_dim = field.shape[-1] // 2
    front_half, back_half = (field[..., :half_dim], field[..., half_dim:])
    return jnp.concatenate([front_half * cosine_table - back_half * sine_table, back_half * cosine_table + front_half * sine_table], axis=-1)

def exact_dot(left, right):
    return jnp.dot(left, right, precision=lax.Precision.HIGHEST)

def norm_unit(values):
    return values * lax.rsqrt(lax.optimization_barrier(jnp.mean(values * values, axis=-1, keepdims=True)) + EPSILON)

def group_layer(params, pieces):
    gain_one, w_query, w_key, w_value, w_out, gain_two, w_gate, w_up, w_down = params
    group_in, group_pos, group_ids = pieces
    group_rows = group_in.shape[0]
    block_rows = min(512, group_rows)
    block_count = group_rows // block_rows
    score_scale = HEAD_DIM ** (-0.5)
    score_bias = -math.log(GROUP_TOK)
    normed1 = low(norm_unit(group_in) * gain_one)
    cosine_table, sine_table = rope_tables(group_pos, HEAD_DIM)
    query = low(rotate(low_back(exact_dot(normed1, w_query)).reshape(group_rows, HEADS, HEAD_DIM), cosine_table, sine_table))
    key = low(rotate(low_back(exact_dot(normed1, w_key)).reshape(group_rows, HEADS, HEAD_DIM), cosine_table, sine_table))
    value = low(low_back(exact_dot(normed1, w_value))).reshape(group_rows, HEADS, HEAD_DIM)
    row_index = jnp.arange(group_rows, dtype=jnp.int32)

    def attend_block(blocked):
        query_block, query_rows, query_ids = blocked
        raw_scores = jnp.einsum('qhd,khd->hqk', query_block, key, precision=lax.Precision.HIGHEST)
        scores = low_back(raw_scores * score_scale + score_bias)
        allowed = (row_index[None, :] <= query_rows[:, None]) & (group_ids[None, :] == query_ids[:, None])
        weights = low(jnp.where(allowed[None], jax.nn.sigmoid(scores), 0.0))
        return jnp.einsum('hqk,khd->qhd', weights, value, precision=lax.Precision.HIGHEST)
    mixed = lax.map(jax.checkpoint(attend_block), (query.reshape(block_count, block_rows, HEADS, HEAD_DIM), row_index.reshape(block_count, block_rows), group_ids.reshape(block_count, block_rows)))
    mixed = low(low_back(mixed.reshape(group_rows, D)))
    residual = group_in + low_back(exact_dot(mixed, w_out))
    normed2 = low(norm_unit(residual) * gain_two)
    gate = low_back(exact_dot(normed2, w_gate))
    upward = low_back(exact_dot(normed2, w_up))
    inner = low(jax.nn.silu(gate) * upward)
    return residual + low_back(exact_dot(inner, w_down))

def reference(inputs, positions, seq_ids, attn_gain, w_query, w_key, w_value, w_out, ffn_gain, w_gate, w_up, w_down, cotangent):
    group_count = TOKENS // GROUP_TOK
    params = [a.astype(jnp.float32) for a in (attn_gain, w_query, w_key, w_value, w_out, ffn_gain, w_gate, w_up, w_down)]
    inputs_float = inputs.astype(jnp.float32)

    def forward(input_rows, *weights):
        layered = jax.checkpoint(group_layer)
        outputs = lax.map(lambda pieces: layered(weights, pieces), (input_rows.reshape(group_count, GROUP_TOK, D), positions.reshape(group_count, GROUP_TOK), seq_ids.reshape(group_count, GROUP_TOK)))
        return outputs.reshape(TOKENS, D)
    output_rows, pullback = jax.vjp(forward, inputs_float, *params)
    grads = pullback(cotangent.astype(jnp.float32))
    return (output_rows.astype(jnp.bfloat16), grads[0], grads[1], grads[2], grads[3], grads[4], grads[5], grads[6], grads[7], grads[8], grads[9])
```

```python
import math

import jax
import jax.numpy as jnp
from jax import lax
from jax.sharding import PartitionSpec as P

HEADS = 16
HEAD_DIM = 128
EPSILON = 1e-05
BOTH = ("seq", "fsdp")
BF = jnp.bfloat16
F32 = jnp.float32


def nn(left, right):
    return lax.dot_general(left, right, (((1,), (0,)), ((), ())), preferred_element_type=F32)


def nt(left, right):
    return lax.dot_general(left, right, (((1,), (1,)), ((), ())), preferred_element_type=F32)


def tn(left, right):
    return lax.dot_general(left, right, (((0,), (0,)), ((), ())), preferred_element_type=F32)


def after(value, *deps):
    return lax.optimization_barrier((value, *deps))[0]


def pick(blocks, index):
    return lax.dynamic_index_in_dim(blocks, index, 0, keepdims=False)


class Net:
    def __init__(self):
        self.ns = lax.axis_size("seq")
        self.nf = lax.axis_size("fsdp")
        self.nz = self.nf // 2
        ns, nf, nz = self.ns, self.nf, self.nz
        half = ns // 2
        self.s_order = list(range(half)) + list(range(ns - 1, half - 1, -1))
        self.z_order = list(range(0, nz, 2)) + list(range(nz - 1 - nz % 2, 0, -2))
        s_next = {self.s_order[i]: self.s_order[(i + 1) % ns] for i in range(ns)}
        s_prev = {b: a for a, b in s_next.items()}
        z_next = {self.z_order[i]: self.z_order[(i + 1) % nz] for i in range(nz)}
        self.s_perm = [
            (s * nf + f, (s_next[s] if f % 2 == 0 else s_prev[s]) * nf + f)
            for f in range(nf)
            for s in range(ns)
        ]
        self.z_perm = [(2 * z + c, 2 * z_next[z] + c) for z in range(nz) for c in range(2)]
        self.c_perm = [(f, f ^ 1) for f in range(nf)]
        self.f = lax.axis_index("fsdp")
        self.s = lax.axis_index("seq")
        self.c = self.f % 2
        self.z = self.f // 2
        s_at = [self.s_order.index(s) for s in range(ns)]
        z_at = [self.z_order.index(z) for z in range(nz)]
        self.s_place = jnp.array(s_at, jnp.int32)[self.s]
        self.z_place = jnp.array(z_at, jnp.int32)[self.z]
        self.s_sign = 1 - 2 * self.c

    def s_back(self, k):
        return jnp.array(self.s_order, jnp.int32)[(self.s_place - self.s_sign * k) % self.ns]

    def z_back(self, k):
        return jnp.array(self.z_order, jnp.int32)[(self.z_place - k) % self.nz]

    def step_s(self, value):
        return lax.ppermute(value, BOTH, self.s_perm)

    def step_z(self, value):
        return lax.ppermute(value, "fsdp", self.z_perm)

    def swap_c(self, value):
        return lax.ppermute(value, "fsdp", self.c_perm)

    def gather_s(self, value, axis=0):
        shape = list(value.shape)
        shape.insert(axis, self.ns)
        out = jnp.zeros(shape, value.dtype)
        held = value
        for k in range(self.ns):
            if k:
                held = self.step_s(held)
            out = lax.dynamic_update_slice_in_dim(
                out, jnp.expand_dims(held, axis), self.s_back(k), axis
            )
        return out

    def gather_f(self, value):
        out = jnp.zeros((self.nz, 2, *value.shape), value.dtype)
        zero = jnp.int32(0)
        rest = (zero,) * value.ndim
        held = value
        for k in range(self.nz):
            if k:
                held = self.step_z(held)
            other = self.swap_c(held)
            row = self.z_back(k)
            out = lax.dynamic_update_slice(out, held[None, None], (row, self.c, *rest))
            out = lax.dynamic_update_slice(out, other[None, None], (row, 1 - self.c, *rest))
        return out.reshape(self.nf, *value.shape)

    def scatter_s(self, part):
        total = part(self.s_back(1))
        for k in range(1, self.ns):
            came = self.step_s(total.astype(BF))
            total = part(self.s_back(k + 1)) + came.astype(F32)
        return total

    def scatter_f(self, blocks):
        pairs = blocks.reshape(self.nz, 2, *blocks.shape[1:])
        away = lax.dynamic_index_in_dim(pairs, 1 - self.c, 1, keepdims=False)
        mine = lax.dynamic_index_in_dim(pairs, self.c, 1, keepdims=False)
        mine = mine.astype(F32) + self.swap_c(away.astype(BF)).astype(F32)
        total = pick(mine, self.z_back(1))
        for k in range(1, self.nz):
            came = self.step_z(total.astype(BF))
            total = pick(mine, self.z_back(k + 1)) + came.astype(F32)
        return total

    def swap_f(self, blocks):
        pairs = blocks.reshape(self.nz, 2, *blocks.shape[1:])
        away = lax.dynamic_index_in_dim(pairs, 1 - self.c, 1, keepdims=False)
        mine = lax.dynamic_index_in_dim(pairs, self.c, 1, keepdims=False)
        came = self.swap_c(away)
        first = jnp.where(self.c == 0, mine, came)
        second = jnp.where(self.c == 0, came, mine)
        both = jnp.stack([first, second], axis=1)
        out = both
        for k in range(1, self.nz):
            perm = [
                (2 * z + c, 2 * ((z + k) % self.nz) + c) for z in range(self.nz) for c in range(2)
            ]
            got = lax.ppermute(pick(both, (self.z + k) % self.nz), "fsdp", perm)
            out = lax.dynamic_update_slice_in_dim(out, got[None], (self.z - k) % self.nz, 0)
        return out.reshape(blocks.shape)

    def swap_s(self, blocks):
        out = blocks
        for k in range(1, self.ns):
            perm = [(s, s ^ k) for s in range(self.ns)]
            got = lax.ppermute(pick(blocks, self.s ^ k), "seq", perm)
            out = lax.dynamic_update_slice_in_dim(out, got[None], self.s ^ k, 0)
        return out


def rotate(field, cosine, sine):
    half = field.shape[-1] // 2
    front, back = field[..., :half], field[..., half:]
    return jnp.concatenate([front * cosine - back * sine, back * cosine + front * sine], axis=-1)


def shards(
    inputs,
    positions,
    seq_ids,
    attn_gain,
    w_query,
    w_key,
    w_value,
    w_out,
    ffn_gain,
    w_gate,
    w_up,
    w_down,
    cotangent,
):
    net = Net()
    ns, nf = net.ns, net.nf
    rows, width = inputs.shape
    group = rows * ns
    own = w_query.shape[0]
    hidden = w_gate.shape[1]
    scale = HEAD_DIM ** (-0.5)
    bias = -math.log(group)
    per_head = HEAD_DIM // own
    swap_head = []
    for f in range(nf):
        for s in range(ns):
            fh, fl = divmod(f, per_head)
            sh, sl = divmod(s, per_head)
            swap_head.append((s * nf + f, (sh * per_head + fl) * nf + fh * per_head + sl))
    heads = HEADS // ns
    cols = heads * HEAD_DIM

    def to_heads(weight):
        view = weight.reshape(own, nf // per_head, per_head, ns // per_head, HEAD_DIM)
        return view.transpose(3, 2, 0, 1, 4).reshape(ns, own, cols)

    def from_heads(blocks):
        view = blocks.reshape(ns // per_head, per_head, own, nf // per_head, HEAD_DIM)
        return view.transpose(2, 3, 1, 0, 4).reshape(own, width)

    gain_one = attn_gain.astype(F32)[:, None]
    gain_two = ffn_gain.astype(F32)[:, None]

    def scaled(weight, gain):
        return (weight.astype(F32) * gain).astype(BF)

    qkv_blocks = jnp.concatenate(
        [to_heads(scaled(w, gain_one)) for w in (w_query, w_key, w_value)], axis=2
    )
    qkv_rows = net.swap_s(qkv_blocks).reshape(ns * own, 3 * cols)
    out_rows = lax.ppermute(w_out, BOTH, swap_head)
    w_qkv = net.gather_f(qkv_rows).reshape(width, 3 * cols)
    w_o = net.gather_f(out_rows).reshape(cols, width)

    input_float = inputs.astype(F32)
    inverse_one = lax.rsqrt(jnp.mean(input_float * input_float, axis=-1, keepdims=True) + EPSILON)
    unit_one = input_float * inverse_one
    unit_all = net.gather_s(unit_one.astype(BF)).reshape(group, width)
    marks = net.gather_s(jnp.stack([positions, seq_ids]))
    places, ids = marks[:, 0].reshape(group), marks[:, 1].reshape(group)

    down_all = net.gather_s(w_down).reshape(hidden // nf, width)
    fcols = hidden // nf

    def spread(weight):
        blocks = weight.reshape(own, nf, fcols).transpose(1, 0, 2)
        return net.gather_s(net.swap_f(blocks), axis=1).reshape(width, fcols)

    gate_src, up_src = after((scaled(w_gate, gain_two), scaled(w_up, gain_two)), w_qkv)
    gate_all = spread(gate_src)
    up_all = spread(up_src)

    frequency = 10000.0 ** (-(jnp.arange(HEAD_DIM // 2, dtype=F32) * 2.0) / HEAD_DIM)
    angles = places.astype(F32)[:, None] * frequency[None, :]
    cosine, sine = jnp.cos(angles)[:, None, :], jnp.sin(angles)[:, None, :]
    qkv = nn(unit_all, w_qkv).reshape(group, 3, heads, HEAD_DIM)
    query = rotate(qkv[:, 0], cosine, sine).astype(BF)
    key = rotate(qkv[:, 1], cosine, sine).astype(BF)
    value = qkv[:, 2].astype(BF)
    index = jnp.arange(group, dtype=jnp.int32)
    allowed = (index[None, :] <= index[:, None]) & (ids[None, :] == ids[:, None])
    raw = jnp.einsum("qhd,khd->hqk", query, key, preferred_element_type=F32)
    weights = jnp.where(allowed[None], jax.nn.sigmoid(raw * scale + bias), 0.0)
    weights_low = weights.astype(BF)
    mixed = jnp.einsum("hqk,khd->qhd", weights_low, value, preferred_element_type=F32)
    mixed = mixed.reshape(group, cols).astype(BF)
    attended = nn(mixed, w_o).reshape(ns, rows, width)
    residual = input_float + net.scatter_s(lambda s: pick(attended, s))

    inverse_two = lax.rsqrt(jnp.mean(residual * residual, axis=-1, keepdims=True) + EPSILON)
    unit_two = residual * inverse_two
    unit2_all = net.gather_f(unit_two.astype(BF)).reshape(nf * rows, width)
    cot_all = net.gather_f(after(cotangent, unit2_all)).reshape(nf * rows, width)
    gate = nn(unit2_all, gate_all)
    upward = nn(unit2_all, up_all)
    sigma = jax.nn.sigmoid(gate)
    inner = (gate * sigma * upward).astype(BF)

    d_inner = nt(cot_all, down_all)
    d_gate = (d_inner * upward * sigma * (1.0 + gate * (1.0 - sigma))).astype(BF)
    d_up = (d_inner * gate * sigma).astype(BF)
    scaled_two = net.scatter_f((nt(d_gate, gate_all) + nt(d_up, up_all)).reshape(nf, rows, width))
    d_residual = cotangent.astype(F32) + inverse_two * (
        scaled_two - unit_two * jnp.mean(scaled_two * unit_two, axis=-1, keepdims=True)
    )
    d_attended = net.gather_s(d_residual.astype(BF)).reshape(group, width)

    out_part = nn(inner, down_all).astype(BF).reshape(nf, rows, width)
    layer_out = (residual + net.scatter_f(after(out_part, d_residual))).astype(BF)

    down_term = tn(inner, cot_all).reshape(ns, hidden // nf // ns, width)
    grad_down = net.scatter_s(lambda s: pick(down_term, s))
    gate_term = tn(unit2_all, d_gate).reshape(nf, ns, own, fcols)
    up_term = tn(unit2_all, d_up).reshape(nf, ns, own, fcols)

    def collect(term):
        mine = net.scatter_s(lambda s: lax.dynamic_index_in_dim(term, s, 1, keepdims=False))
        blocks = net.swap_f(mine.astype(BF))
        return blocks.transpose(1, 0, 2).reshape(own, hidden).astype(F32)

    plain_gate = collect(gate_term)
    plain_up = collect(up_term)
    grad_ffn_gain = jnp.sum(
        w_gate.astype(F32) * plain_gate + w_up.astype(F32) * plain_up, axis=1
    )

    d_mixed = nt(d_attended, w_o).astype(BF).reshape(group, heads, HEAD_DIM)
    out_term = tn(mixed, d_attended).reshape(nf, own, width)
    d_weights = jnp.einsum("qhd,khd->hqk", d_mixed, value, preferred_element_type=F32)
    d_scores = (d_weights * weights * (1.0 - weights)).astype(BF)
    d_query = jnp.einsum("hqk,khd->qhd", d_scores, key, preferred_element_type=F32) * scale
    d_key = jnp.einsum("hqk,qhd->khd", d_scores, query, preferred_element_type=F32) * scale
    d_value = jnp.einsum("hqk,qhd->khd", weights_low, d_mixed, preferred_element_type=F32)
    d_qkv = jnp.concatenate(
        [
            rotate(d_query, cosine, -sine).astype(BF).reshape(group, cols),
            rotate(d_key, cosine, -sine).astype(BF).reshape(group, cols),
            d_value.astype(BF).reshape(group, cols),
        ],
        axis=1,
    )
    norm_term = nt(d_qkv, w_qkv).reshape(ns, rows, width)
    scaled_one = net.scatter_s(lambda s: pick(norm_term, s))
    grad_input = d_residual + inverse_one * (
        scaled_one - unit_one * jnp.mean(scaled_one * unit_one, axis=-1, keepdims=True)
    )
    qkv_term = tn(unit_all, d_qkv).reshape(nf, ns * own, 3 * cols)
    qkv_mine = net.scatter_f(qkv_term).astype(BF).reshape(ns, own, 3 * cols)
    qkv_own = net.swap_s(qkv_mine).astype(F32)
    plain_query, plain_key, plain_value = (
        from_heads(qkv_own[:, :, i * cols : (i + 1) * cols]) for i in range(3)
    )
    grad_attn_gain = jnp.sum(
        w_query.astype(F32) * plain_query
        + w_key.astype(F32) * plain_key
        + w_value.astype(F32) * plain_value,
        axis=1,
    )
    out_mine = net.scatter_f(out_term).astype(BF)
    back_head = [(b, a) for a, b in swap_head]
    grad_out = lax.ppermute(out_mine, BOTH, back_head).astype(F32)
    return (
        layer_out,
        grad_input,
        grad_attn_gain,
        plain_query * gain_one,
        plain_key * gain_one,
        plain_value * gain_one,
        grad_out,
        grad_ffn_gain,
        plain_gate * gain_two,
        plain_up * gain_two,
        grad_down,
    )


def solution(mesh):
    row = P(("fsdp", "seq"), None)
    flat = P(("fsdp", "seq"))
    return jax.shard_map(
        shards,
        mesh=mesh,
        in_specs=(row, flat, flat, flat, row, row, row, row, flat, row, row, row, row),
        out_specs=(row, row, flat, row, row, row, row, flat, row, row, row),
        check_vma=False,
    )
```

```python
import functools
import math

import jax
import jax.numpy as jnp
from jax import lax
from jax.experimental import pallas as pl
from jax.experimental.pallas import tpu as pltpu
from jax.sharding import PartitionSpec as P

HEADS = 16
HEAD_DIM = 128
EPSILON = 1e-05
BOTH = ("seq", "fsdp")
BF = jnp.bfloat16
F32 = jnp.float32
TILE = 256
EXTRA = 16
FTILE = 512
VMEM_LIMIT = 56 * 1024 * 1024
PARAMS = pltpu.CompilerParams(vmem_limit_bytes=VMEM_LIMIT)
FFN_PARAMS = pltpu.CompilerParams(vmem_limit_bytes=48 * 1024 * 1024)
WHOLE = pl.BlockSpec(memory_space=pltpu.VMEM)


def nn(left, right):
    return lax.dot_general(left, right, (((1,), (0,)), ((), ())), preferred_element_type=F32)


def nt(left, right):
    return lax.dot_general(left, right, (((1,), (1,)), ((), ())), preferred_element_type=F32)


def tn(left, right):
    return lax.dot_general(left, right, (((0,), (0,)), ((), ())), preferred_element_type=F32)


def after(value, *deps):
    return lax.optimization_barrier((value, *deps))[0]


def shape_of(*dims, dtype=BF):
    return jax.ShapeDtypeStruct(dims, dtype)


def cost(flops, moved):
    return pl.CostEstimate(flops=int(flops), bytes_accessed=int(moved), transcendentals=0)


class Net:
    def __init__(self):
        self.ns = lax.axis_size("seq")
        self.nf = lax.axis_size("fsdp")
        self.nz = self.nf // 2
        ns, nf, nz = self.ns, self.nf, self.nz
        half = ns // 2
        self.s_order = list(range(half)) + list(range(ns - 1, half - 1, -1))
        self.z_order = list(range(0, nz, 2)) + list(range(nz - 1 - nz % 2, 0, -2))
        s_next = {self.s_order[i]: self.s_order[(i + 1) % ns] for i in range(ns)}
        s_prev = {b: a for a, b in s_next.items()}
        z_next = {self.z_order[i]: self.z_order[(i + 1) % nz] for i in range(nz)}
        self.s_perm = [
            (s * nf + f, (s_next[s] if f % 2 == 0 else s_prev[s]) * nf + f)
            for f in range(nf)
            for s in range(ns)
        ]
        self.z_perm = [(2 * z + c, 2 * z_next[z] + c) for z in range(nz) for c in range(2)]
        self.c_perm = [(f, f ^ 1) for f in range(nf)]
        self.f = lax.axis_index("fsdp")
        self.s = lax.axis_index("seq")
        self.c = self.f % 2
        self.z = self.f // 2
        self.s_place = self.fold(self.s)
        self.z_place = jnp.where(self.z % 2 == 0, self.z // 2, nz - 1 - self.z // 2)
        self.s_sign = 1 - 2 * self.c

    def fold(self, value):
        half = self.ns // 2
        return jnp.where(value < half, value, self.ns - 1 + half - value)

    def s_back(self, k):
        return self.fold((self.s_place - self.s_sign * k + self.ns) % self.ns)

    def z_back(self, k):
        place = (self.z_place - k + self.nz) % self.nz
        return jnp.where(2 * place < self.nz, 2 * place, 2 * (self.nz - 1 - place) + 1)

    def step_s(self, value):
        return lax.ppermute(value, BOTH, self.s_perm)

    def step_z(self, value):
        return lax.ppermute(value, "fsdp", self.z_perm)

    def swap_c(self, value):
        return lax.ppermute(value, "fsdp", self.c_perm)

    def ring_s(self, value):
        blocks = [value]
        for _ in range(1, self.ns):
            blocks.append(self.step_s(blocks[-1]))
        return blocks

    def ring_f(self, value):
        held, blocks = value, []
        for k in range(self.nz):
            if k:
                held = self.step_z(held)
            blocks += [held, self.swap_c(held)]
        return blocks

    def origin_f(self):
        out = []
        for k in range(self.nz):
            out += [self.z_back(k) * 2 + self.c, self.z_back(k) * 2 + 1 - self.c]
        return jnp.stack(out).astype(jnp.int32)

    def swap_s(self, blocks):
        out = blocks
        for k in range(1, self.ns):
            perm = [(s, s ^ k) for s in range(self.ns)]
            piece = lax.dynamic_index_in_dim(blocks, self.s ^ k, 0, keepdims=True)
            got = lax.ppermute(piece, "seq", perm)
            out = lax.dynamic_update_slice_in_dim(out, got, self.s ^ k, 0)
        return out

    def natural_s(self, blocks):
        out = jnp.zeros((self.ns, *blocks[0].shape), blocks[0].dtype)
        for k, block in enumerate(blocks):
            out = lax.dynamic_update_slice_in_dim(out, block[None], self.s_back(k), 0)
        return out

    def scatter_s(self, parts, gate=lambda k, value: value):
        came = None
        for k in range(1, self.ns):
            total = parts[k] if came is None else parts[k].astype(F32) + came.astype(F32)
            came = self.step_s(gate(k, total.astype(BF)))
        return parts[0], came

    def scatter_f(self, part, gate=lambda k, value, sent: value):
        came, sent = None, []
        for k in range(1, self.nz + 1):
            mine, away = part(k % self.nz, sent)
            other = self.swap_c(away)
            if k == self.nz:
                return (mine, other, came), sent
            total = mine.astype(F32) + other.astype(F32)
            if came is not None:
                total = total + came.astype(F32)
            sent.append(gate(k, total.astype(BF), sent))
            came = self.step_z(sent[-1])


def split(values, count):
    return tuple(values[:count]), list(values[count:])


def total_of(terms):
    return sum(term.astype(F32) for term in terms)


def pack_ffn_kernel(fcols, gate_ref, up_ref, out_ref):
    for i in range(gate_ref.shape[1] // fcols):
        for t in range(fcols // FTILE):
            here = slice(i * fcols + t * FTILE, i * fcols + (t + 1) * FTILE)
            out_ref[i, :, 2 * t * FTILE : (2 * t + 1) * FTILE] = gate_ref[:, here]
            out_ref[i, :, (2 * t + 1) * FTILE : (2 * t + 2) * FTILE] = up_ref[:, here]


def pack_ffn(w_gate, w_up, nf):
    own, hidden = w_gate.shape
    fcols = hidden // nf
    return pl.pallas_call(
        functools.partial(pack_ffn_kernel, fcols),
        grid=(nf // 2,),
        in_specs=[pl.BlockSpec((own, 2 * fcols), lambda i: (0, i))] * 2,
        out_specs=pl.BlockSpec((2, own, 2 * fcols), lambda i: (i, 0, 0)),
        out_shape=shape_of(nf, own, 2 * fcols),
    )(w_gate, w_up)


def unpack_ffn_kernel(fcols, w_gate_ref, w_up_ref, gain_ref, in_ref, *out_refs):
    gate_ref, up_ref, gain_out_ref = out_refs
    total = jnp.zeros(gain_out_ref.shape, F32)
    for t in range(fcols // FTILE):
        here = slice(t * FTILE, (t + 1) * FTILE)
        gate = in_ref[0, :, 2 * t * FTILE : (2 * t + 1) * FTILE].astype(F32)
        upward = in_ref[0, :, (2 * t + 1) * FTILE : (2 * t + 2) * FTILE].astype(F32)
        gate_ref[:, here] = gate
        up_ref[:, here] = upward
        both = gate * w_gate_ref[:, here].astype(F32) + upward * w_up_ref[:, here].astype(F32)
        total = total + jnp.sum(both, axis=1, keepdims=True)

    @pl.when(pl.program_id(0) == 0)
    def _():
        gain_out_ref[...] = jnp.zeros_like(gain_out_ref)

    gain_out_ref[...] += total / gain_ref[...]


def unpack_ffn(w_gate, w_up, gain, blocks):
    own, hidden = w_gate.shape
    nf = blocks.shape[0]
    fcols = hidden // nf
    wide = pl.BlockSpec((own, fcols), lambda i: (0, i))
    thin = pl.BlockSpec((own, 1), lambda i: (0, 0))
    gate, upward, grad_gain = pl.pallas_call(
        functools.partial(unpack_ffn_kernel, fcols),
        grid=(nf,),
        in_specs=[wide, wide, thin, pl.BlockSpec((1, own, 2 * fcols), lambda i: (i, 0, 0))],
        out_specs=[wide, wide, thin],
        out_shape=[
            shape_of(own, hidden, dtype=F32),
            shape_of(own, hidden, dtype=F32),
            shape_of(own, 1, dtype=F32),
        ],
    )(w_gate, w_up, gain, blocks)
    return gate, upward, grad_gain[:, 0]


def head_of(s, j, ns, nf, per_head):
    sh, fl = divmod(s, per_head)
    return (j * per_head + fl) * (ns // per_head) + sh


def pack_heads_kernel(ns, nf, per_head, *refs):
    *in_refs, extra_ref, out_ref = refs
    heads = HEADS // ns
    own = in_refs[0].shape[0]
    for s in range(ns):
        out_ref[s, own:, :] = jnp.zeros((EXTRA, out_ref.shape[2]), BF)
        out_ref[s, own:, : extra_ref.shape[1]] = extra_ref[...]
        for i, ref in enumerate(in_refs):
            for j in range(heads):
                h = head_of(s, j, ns, nf, per_head)
                at = (i * heads + j) * HEAD_DIM
                out_ref[s, :own, at : at + HEAD_DIM] = ref[:, h * HEAD_DIM : (h + 1) * HEAD_DIM]


def pack_heads(weights, extra, ns, nf, per_head):
    own, width = weights[0].shape
    return pl.pallas_call(
        functools.partial(pack_heads_kernel, ns, nf, per_head),
        in_specs=[WHOLE] * 4,
        out_specs=WHOLE,
        out_shape=shape_of(ns, own + EXTRA, 3 * width // ns),
        compiler_params=PARAMS,
    )(*weights, extra)


def unpack_heads_kernel(ns, nf, per_head, in_ref, gain_ref, *refs):
    weight_refs, grad_refs, gain_out_ref = refs[:3], refs[3:6], refs[6]
    heads = HEADS // ns
    total = jnp.zeros(gain_out_ref.shape, F32)
    for s in range(ns):
        for i in range(3):
            for j in range(heads):
                h = head_of(s, j, ns, nf, per_head)
                at = (i * heads + j) * HEAD_DIM
                here = slice(h * HEAD_DIM, (h + 1) * HEAD_DIM)
                grad = in_ref[s, :, at : at + HEAD_DIM].astype(F32)
                grad_refs[i][:, here] = grad
                total = total + jnp.sum(
                    grad * weight_refs[i][:, here].astype(F32), axis=1, keepdims=True
                )
    gain_out_ref[...] = total / gain_ref[...]


def unpack_heads(blocks, gain, weights, ns, nf, per_head):
    own, width = weights[0].shape
    *grads, grad_gain = pl.pallas_call(
        functools.partial(unpack_heads_kernel, ns, nf, per_head),
        in_specs=[WHOLE] * 5,
        out_specs=[WHOLE] * 4,
        out_shape=[shape_of(own, width, dtype=F32)] * 3 + [shape_of(own, 1, dtype=F32)],
        compiler_params=PARAMS,
    )(blocks, gain, *weights)
    return *grads, grad_gain[:, 0]


def spin(field, cosine, sine):
    return field * cosine + pltpu.roll(field, HEAD_DIM // 2, 1) * sine


def lay_out_weight(origin_ref, blocks, start, own, ns, out_ref):
    piece = out_ref.shape[1] // ns
    for j, block in enumerate(blocks):
        row = pl.multiple_of(origin_ref[j] * own, own)
        for q in range(ns):
            out_ref[pl.ds(row, own), q * piece : (q + 1) * piece] = block[
                q * own : (q + 1) * own, start:
            ]


def weights_of(scores, scale, bias, mask):
    return jnp.where(mask, jax.nn.sigmoid(scores * scale + bias), 0.0)


def mask_of(col_ref, row_ref):
    return (row_ref[0:1, :] <= col_ref[:, 0:1]) & (row_ref[1:2, :] == col_ref[:, 1:2])


def attend_kernel(
    dims, origin_ref, input_ref, inverse_ref, cos_ref, sin_ref, col_ref, row_ref, *refs
):
    ns, nf, own, cols, scale, bias = dims
    blocks = refs[:nf]
    q_ref, k_ref, v_ref, mixed_ref, att_ref, normed_ref, gains_ref, out_w = refs[nf:]
    deep = ns * own
    lay_out_weight(origin_ref, blocks, 3 * cols, own, ns, out_w)
    for j, block in enumerate(blocks):
        here = pl.ds(pl.multiple_of(origin_ref[j] * deep, deep), deep)
        gains = block[deep : deep + EXTRA, :deep].astype(F32)
        gains_ref[:, here] = gains
        unit = input_ref[:, here].astype(F32) * inverse_ref[...]
        normed_ref[:, here] = (unit * gains[0:1, :]).astype(BF)
    for part, ref in enumerate((q_ref, k_ref, v_ref)):

        @pl.loop(0, cols // TILE)
        def _(t, part=part, ref=ref):
            at = pl.multiple_of(part * cols + t * TILE, TILE)
            total = None
            for j, block in enumerate(blocks):
                from_col = pl.multiple_of(origin_ref[j] * deep, deep)
                term = nn(normed_ref[:, pl.ds(from_col, deep)], block[:deep, pl.ds(at, TILE)])
                total = term if total is None else total + term
            for i in range(TILE // HEAD_DIM):
                field = total[:, i * HEAD_DIM : (i + 1) * HEAD_DIM]
                if part < 2:
                    field = spin(field, cos_ref[...], sin_ref[...])
                to = pl.multiple_of(t * TILE + i * HEAD_DIM, HEAD_DIM)
                ref[:, pl.ds(to, HEAD_DIM)] = field.astype(BF)

    mask = mask_of(col_ref, row_ref)

    @pl.loop(0, cols // HEAD_DIM)
    def _(h):
        here = pl.ds(pl.multiple_of(h * HEAD_DIM, HEAD_DIM), HEAD_DIM)
        weights = weights_of(nt(q_ref[:, here], k_ref[:, here]), scale, bias, mask)
        mixed_ref[:, here] = nn(weights.astype(BF), v_ref[:, here]).astype(BF)

    wide = 512

    @pl.loop(0, att_ref.shape[1] // wide)
    def _(t):
        here = pl.ds(pl.multiple_of(t * wide, wide), wide)
        att_ref[:, here] = nn(mixed_ref[...], out_w[:, here]).astype(BF)


def attend(dims, origin, rows, inverse, tables, marks, blocks):
    ns, nf, own, cols, _, _ = dims
    group, width = rows.shape
    small = shape_of(group, cols)
    return pl.pallas_call(
        functools.partial(attend_kernel, dims),
        in_specs=[pl.BlockSpec(memory_space=pltpu.SMEM)] + [WHOLE] * (6 + nf),
        out_specs=[WHOLE] * 7,
        out_shape=[small] * 4
        + [shape_of(group, width)] * 2
        + [shape_of(EXTRA, width, dtype=F32)],
        scratch_shapes=[pltpu.VMEM((cols, width), BF)],
        compiler_params=PARAMS,
        cost_estimate=cost(
            2 * group * width * cols * 4 + 4 * group * group * cols, 2 * width * cols * 4
        ),
    )(origin, rows, inverse, *tables, *marks, *blocks)


def attend_back_kernel(
    dims, origin_ref, datt_ref, q_ref, k_ref, v_ref, mixed_ref, cos_ref, sin_ref, col_ref, row_ref,
    *refs
):
    ns, nf, own, cols, scale, bias = dims
    blocks = refs[:nf]
    d_qkv, out_term, out_w = refs[nf:]
    piece = datt_ref.shape[1] // ns
    lay_out_weight(origin_ref, blocks, 0, own, ns, out_w)
    mask = mask_of(col_ref, row_ref)

    @pl.loop(0, cols // HEAD_DIM)
    def _(h):
        start = pl.multiple_of(h * HEAD_DIM, HEAD_DIM)
        here = pl.ds(start, HEAD_DIM)
        query, key = q_ref[:, here], k_ref[:, here]
        d_mixed = nt(datt_ref[...], out_w[here, :]).astype(BF)
        weights = weights_of(nt(query, key), scale, bias, mask)
        d_weights = nt(d_mixed, v_ref[:, here])
        d_scores = (d_weights * weights * (1.0 - weights)).astype(BF)
        d_query = nn(d_scores, key) * scale
        d_key = tn(d_scores, query) * scale
        d_value = tn(weights.astype(BF), d_mixed)
        d_qkv[:, here] = spin(d_query, cos_ref[...], -sin_ref[...]).astype(BF)
        d_qkv[:, pl.ds(pl.multiple_of(cols + start, HEAD_DIM), HEAD_DIM)] = spin(
            d_key, cos_ref[...], -sin_ref[...]
        ).astype(BF)
        d_qkv[:, pl.ds(pl.multiple_of(2 * cols + start, HEAD_DIM), HEAD_DIM)] = d_value.astype(BF)

    @pl.loop(0, ns)
    def _(q):
        here = pl.ds(pl.multiple_of(q * piece, piece), piece)
        out_term[q] = tn(mixed_ref[...], datt_ref[:, here]).astype(BF)


def attend_back(dims, origin, datt, saved, tables, marks, blocks):
    ns, nf, own, cols, _, _ = dims
    group, width = datt.shape
    piece = width // ns
    last = pl.BlockSpec((ns * own, piece), lambda i: (0, 3 * cols // piece))

    def full(*shape):
        return pl.BlockSpec(shape, lambda i: (0,) * len(shape))

    arrays = [datt, *saved, *tables, *marks]
    return pl.pallas_call(
        functools.partial(attend_back_kernel, dims),
        grid=(1,),
        in_specs=[pl.BlockSpec(memory_space=pltpu.SMEM)]
        + [full(*array.shape) for array in arrays]
        + [last] * nf,
        out_specs=[full(group, 3 * cols), full(ns, cols, piece)],
        out_shape=[shape_of(group, 3 * cols), shape_of(ns, cols, piece)],
        scratch_shapes=[pltpu.VMEM((cols, width), BF)],
        compiler_params=PARAMS,
        cost_estimate=cost(
            2 * group * width * cols * 2 + 10 * group * group * cols, 4 * width * cols
        ),
    )(origin, *arrays, *blocks)


def weight_grad_kernel(dims, step, origin_ref, normed_ref, d_ref, out_ref, mine_ref, away_ref):
    ns, nf, own, cols, _, _ = dims
    deep = ns * own
    for i, ref in enumerate((mine_ref, away_ref)):
        origin = origin_ref[2 * step + i]
        here = pl.ds(pl.multiple_of(origin * deep, deep), deep)
        ref[:, : 3 * cols] = tn(normed_ref[:, here], d_ref[...]).astype(BF)
        row = pl.multiple_of(origin * own, own)
        for q in range(ns):
            ref[q * own : (q + 1) * own, 3 * cols :] = out_ref[q, pl.ds(row, own), :]


def weight_grad(dims, step, origin, normed, d_qkv, out_term):
    ns, nf, own, cols, _, _ = dims
    term = shape_of(ns * own, 3 * cols + out_term.shape[2])
    return pl.pallas_call(
        functools.partial(weight_grad_kernel, dims, step),
        in_specs=[pl.BlockSpec(memory_space=pltpu.SMEM)] + [WHOLE] * 3,
        out_specs=[WHOLE] * 2,
        out_shape=[term, term],
        compiler_params=PARAMS,
        cost_estimate=cost(12 * normed.shape[0] * ns * own * cols, 2**23),
    )(origin, normed, d_qkv, out_term)


def input_grad_kernel(dims, origin_ref, d_ref, *refs):
    ns, nf, own, cols, _, _ = dims
    *blocks, dn_ref = refs
    deep = ns * own
    for j, block in enumerate(blocks):
        here = pl.ds(pl.multiple_of(origin_ref[j] * deep, deep), deep)
        dn_ref[:, here] = nt(d_ref[...], block[:deep, : 3 * cols]).astype(BF)


def input_grad(dims, origin, d_qkv, blocks, width):
    ns, nf, own, cols, _, _ = dims
    group = d_qkv.shape[0]
    return pl.pallas_call(
        functools.partial(input_grad_kernel, dims),
        in_specs=[pl.BlockSpec(memory_space=pltpu.SMEM)] + [WHOLE] * (1 + nf),
        out_specs=WHOLE,
        out_shape=shape_of(group, width),
        compiler_params=PARAMS,
        cost_estimate=cost(6 * group * width * cols, 8 * width * cols),
    )(origin, d_qkv, *blocks)


def ffn_kernel(count, first, *refs):
    unit_refs, cot_refs, refs = refs[:count], refs[count : 2 * count], refs[2 * count :]
    weight_ref, down_ref = refs[:2]
    refs = refs[2 if first else 6 :]
    inner_ref, d_ref, unit_ref, cot_ref = refs[:4]
    two_refs, out_refs, two, out = refs[4 : 4 + count], refs[4 + count : 4 + 2 * count], *refs[-2:]
    rows = unit_refs[0].shape[0]
    j = pl.program_id(0)

    @pl.when(j == 0)
    def _():
        for i in range(count):
            unit_ref[i * rows : (i + 1) * rows, :] = unit_refs[i][...]
            cot_ref[i * rows : (i + 1) * rows, :] = cot_refs[i][...]

    both = nn(unit_ref[...], weight_ref[...])
    d_inner = nt(cot_ref[...], down_ref[...])
    gate, upward = both[:, :FTILE], both[:, FTILE:]
    sigma = jax.nn.sigmoid(gate)
    silu = gate * sigma
    inner_ref[...] = (silu * upward).astype(BF)
    d_ref[:, :FTILE] = (d_inner * upward * sigma * (1.0 + gate * (1.0 - sigma))).astype(BF)
    d_ref[:, FTILE:] = (d_inner * silu).astype(BF)
    two_term = nt(d_ref[...], weight_ref[...])
    out_term = nn(inner_ref[...], down_ref[...])

    @pl.when(j == 0)
    def _():
        two[...] = two_term
        out[...] = out_term

    @pl.when(j > 0)
    def _():
        two[...] += two_term
        out[...] += out_term

    @pl.when(j == pl.num_programs(0) - 1)
    def _():
        for i in range(count):
            two_refs[i][...] = two[i * rows : (i + 1) * rows, :].astype(BF)
            out_refs[i][...] = out[i * rows : (i + 1) * rows, :].astype(BF)


def ffn(turn, turns, units, cots, weight, down, before):
    rows, width = units[0].shape
    count = len(units)
    fcols = down.shape[0]
    all_rows = count * rows
    whole = pl.BlockSpec((rows, width), lambda j: (0, 0))
    shared = [
        ((all_rows, FTILE), lambda j: (turn, j), fcols),
        ((all_rows, 2 * FTILE), lambda j: (turn, j), 2 * fcols),
        ((all_rows, width), lambda j: (turn, 0), width),
        ((all_rows, width), lambda j: (turn, 0), width),
    ]
    return pl.pallas_call(
        functools.partial(ffn_kernel, count, not before),
        grid=(fcols // FTILE,),
        in_specs=[whole] * (2 * count)
        + [
            pl.BlockSpec((width, 2 * FTILE), lambda j: (0, j)),
            pl.BlockSpec((FTILE, width), lambda j: (j, 0)),
        ]
        + [pl.BlockSpec(memory_space=pl.ANY)] * len(before),
        out_specs=[pl.BlockSpec(shape, at) for shape, at, _ in shared] + [whole] * (2 * count),
        out_shape=[shape_of(turns * all_rows, last) for _, _, last in shared]
        + [shape_of(rows, width)] * (2 * count),
        scratch_shapes=[pltpu.VMEM((all_rows, width), F32)] * 2,
        input_output_aliases={2 * count + 2 + i: i for i in range(len(before))},
        compiler_params=FFN_PARAMS,
        cost_estimate=cost(
            12 * all_rows * width * fcols, 2 * (3 * fcols + 4 * all_rows) * width
        ),
    )(*units, *cots, weight, down, *before)


def norm_two_kernel(ns, nf, own, input_ref, part_ref, came_ref, gain_ref, *out_refs):
    residual_ref, inverse_ref, unit_ref = out_refs
    residual = (
        input_ref[...].astype(F32) + part_ref[...].astype(F32) + came_ref[...].astype(F32)
    )
    inverse = lax.rsqrt(jnp.mean(residual * residual, axis=-1, keepdims=True) + EPSILON)
    residual_ref[...] = residual
    inverse_ref[...] = inverse
    normed = (residual * inverse * gain_ref[...]).astype(BF)
    for f in range(nf):
        for s in range(ns):
            here, there = (f * ns + s) * own, (s * nf + f) * own
            unit_ref[:, there : there + own] = normed[:, here : here + own]


def norm_two(ns, nf, own, rows, part, came, gain):
    count, width = rows.shape
    return pl.pallas_call(
        functools.partial(norm_two_kernel, ns, nf, own),
        in_specs=[WHOLE] * 4,
        out_specs=[WHOLE] * 3,
        out_shape=[
            shape_of(count, width, dtype=F32),
            shape_of(count, 1, dtype=F32),
            shape_of(count, width),
        ],
        compiler_params=PARAMS,
    )(rows, part, came, gain)


def norm_two_back_kernel(ns, nf, own, *refs):
    term_refs, (residual_ref, inverse_ref, gain_ref, cot_ref) = refs[:3], refs[3:7]
    d_ref, low_ref, scaled = refs[7:]
    total = term_refs[0][...].astype(F32)
    for ref in term_refs[1:]:
        total = total + ref[...].astype(F32)
    for f in range(nf):
        for s in range(ns):
            here, there = (f * ns + s) * own, (s * nf + f) * own
            scaled[:, here : here + own] = total[:, there : there + own]
    unit = residual_ref[...] * inverse_ref[...]
    back = scaled[...] * gain_ref[...]
    mean = jnp.mean(back * unit, axis=-1, keepdims=True)
    d_residual = cot_ref[...].astype(F32) + inverse_ref[...] * (back - unit * mean)
    d_ref[...] = d_residual
    low_ref[...] = d_residual.astype(BF)


def norm_two_back(ns, nf, own, terms, residual, inverse, gain, cot):
    count, width = residual.shape
    return pl.pallas_call(
        functools.partial(norm_two_back_kernel, ns, nf, own),
        in_specs=[WHOLE] * 7,
        out_specs=[WHOLE] * 2,
        out_shape=[shape_of(count, width, dtype=F32), shape_of(count, width)],
        scratch_shapes=[pltpu.VMEM((count, width), F32)],
        compiler_params=PARAMS,
    )(*terms, residual, inverse, gain, cot)


def shards(
    inputs,
    positions,
    seq_ids,
    attn_gain,
    w_query,
    w_key,
    w_value,
    w_out,
    ffn_gain,
    w_gate,
    w_up,
    w_down,
    cotangent,
):
    net = Net()
    ns, nf, nz = net.ns, net.nf, net.nz
    rows, width = inputs.shape
    group = rows * ns
    own = w_query.shape[0]
    hidden = w_gate.shape[1]
    fcols = hidden // nf
    per_head = HEAD_DIM // own
    swap_head = []
    for f in range(nf):
        for s in range(ns):
            fh, fl = divmod(f, per_head)
            sh, sl = divmod(s, per_head)
            swap_head.append((s * nf + f, (sh * per_head + fl) * nf + fh * per_head + sl))
    cols = HEADS // ns * HEAD_DIM
    piece = width // ns
    dims = (ns, nf, own, cols, HEAD_DIM ** (-0.5), -math.log(group))

    origin = net.origin_f()
    extra = jnp.stack(
        [
            (positions // 256).astype(BF),
            (positions % 256).astype(BF),
            seq_ids.astype(BF),
            jnp.pad(jnp.concatenate([attn_gain, ffn_gain]), (0, rows - 2 * own)),
        ]
    )
    extra = jnp.pad(extra, ((0, EXTRA - 4), (0, 0)))

    down_all = lax.all_gather(w_down, "seq", axis=0, tiled=True)
    packed_ffn = pack_ffn(w_gate, w_up, nf)
    ffn_rows = lax.all_to_all(packed_ffn, "fsdp", split_axis=0, concat_axis=0, tiled=True)
    packed = pack_heads((w_query, w_key, after(w_value, packed_ffn)), extra, ns, nf, per_head)
    qkv_rows = net.swap_s(packed)
    out_rows = lax.ppermute(w_out, BOTH, swap_head)
    input_ring = net.ring_s(inputs)
    marks = qkv_rows[:, own : own + 4, :rows].astype(F32)
    gain_rows = marks[:, 3, : 2 * own].reshape(ns, 2, own).transpose(1, 0, 2).reshape(2, ns * own)
    merged = jnp.concatenate(
        [
            qkv_rows[:, :own].reshape(ns * own, 3 * cols),
            out_rows.reshape(own, ns, piece).transpose(1, 0, 2).reshape(ns * own, piece),
        ],
        axis=1,
    )
    merged = jnp.concatenate(
        [
            merged,
            jnp.pad(gain_rows.astype(BF), ((0, EXTRA - 2), (0, 3 * cols + piece - ns * own))),
        ],
        axis=0,
    )
    blocks = net.ring_f(merged)
    w_ffn = lax.all_gather(
        after(ffn_rows, blocks[2]).reshape(nf * own, 2 * fcols), "seq", axis=0, tiled=True
    )

    input_all = jnp.concatenate(input_ring, axis=0)
    squares = jnp.mean(jnp.square(input_all.astype(F32)), axis=-1, keepdims=True)
    inverse_all = lax.rsqrt(squares + EPSILON)
    input_float = inputs.astype(F32)
    inverse_one = inverse_all[:rows]
    unit_one = input_float * inverse_one
    order = [net.s_back(k) for k in range(ns)]
    marks = jnp.stack([lax.dynamic_index_in_dim(marks, s, 0, keepdims=False) for s in order])
    places = (marks[:, 0] * 256.0 + marks[:, 1]).reshape(group)
    ids = marks[:, 2].reshape(group)
    index = jnp.concatenate([(s * rows + jnp.arange(rows)).astype(F32) for s in order])
    frequency = 10000.0 ** (-(jnp.arange(HEAD_DIM // 2, dtype=F32) * 2.0) / HEAD_DIM)
    angles = places[:, None] * frequency[None, :]
    cosine, sine = jnp.cos(angles), jnp.sin(angles)
    tables = (
        jnp.concatenate([cosine, cosine], axis=1),
        jnp.concatenate([-sine, sine], axis=1),
    )
    row_marks = jnp.stack([index, ids])
    pair_marks = (row_marks.T, row_marks)

    *saved, attended, normed_all, gains = attend(
        dims, origin, input_all, inverse_all, tables, pair_marks, blocks
    )
    gain_one, gain_two = gains[0:1], gains[1:2]
    cots = net.ring_f(after(cotangent, blocks[-2]))
    att_terms = net.scatter_s(
        attended.reshape(ns, rows, width),
        lambda k, value: after(value, cots[2 * k]) if k < nz else value,
    )

    residual, inverse_two, unit_low = norm_two(ns, nf, own, inputs, *att_terms, gain_two)
    unit_two = residual * inverse_two
    units = net.ring_f(unit_low)
    shared, two_parts, out_parts = (), [], []
    turns = nz // 2
    each = 2 * nz // turns
    for turn in range(turns):
        here = slice(each * turn, each * (turn + 1))
        shared, done = split(
            ffn(turn, turns, units[here], cots[here], w_ffn, down_all, shared), 4
        )
        two_parts += done[:each]
        out_parts += done[each:]
    inner, d_ffn, unit_all, cot_all = shared
    sums = {}

    def two_gate(k, value, sent):
        if k == 2:
            sums["ffn"] = tn(after(unit_all, sent[0]), d_ffn).astype(BF)
            return after(value, sums["ffn"])
        if k == 3:
            sums["down"] = tn(after(inner, sent[1]), cot_all).astype(BF)
            return after(value, sums["down"])
        return value

    two_terms, two_sent = net.scatter_f(lambda k, sent: two_parts[2 * k : 2 * k + 2], two_gate)
    d_residual, d_low = norm_two_back(
        ns, nf, own, two_terms, residual, inverse_two, gain_two, cotangent
    )
    d_attended = net.ring_s(d_low)
    ffn_sum = lax.psum_scatter(
        sums["ffn"].reshape(ns, nf * own, 2 * fcols), "seq", scatter_dimension=0, tiled=False
    )
    grad_down = lax.psum_scatter(
        after(sums["down"], ffn_sum), "seq", scatter_dimension=0, tiled=True
    ).astype(F32)
    out_terms, out_sent = net.scatter_f(
        lambda k, sent: out_parts[2 * k : 2 * k + 2],
        lambda k, value, sent: after(value, d_attended[k]) if k < ns else value,
    )
    layer_out = (residual + total_of(out_terms)).astype(BF)
    ffn_own = lax.all_to_all(
        ffn_sum.reshape(nf, own, 2 * fcols), "fsdp", split_axis=0, concat_axis=0, tiled=True
    )
    grad_gate, grad_up, grad_ffn_gain = unpack_ffn(
        w_gate,
        w_up,
        ffn_gain.astype(F32)[:, None],
        ffn_own,
    )

    d_qkv, out_grad = attend_back(
        dims, origin, jnp.concatenate(d_attended, axis=0), saved, tables, pair_marks, blocks
    )
    held = {}

    def weight_part(k, sent):
        if k == 1:
            ready = after(d_qkv, out_terms[2])
        else:
            ready = after(d_qkv, sent[min(len(sent), 2) - 1])
        return weight_grad(dims, k, origin, normed_all, ready, out_grad)

    def weight_gate(k, value, sent):
        if k == 2:
            dn_parts = input_grad(dims, origin, after(d_qkv, sent[0]), blocks, width)
            held["one"] = total_of(net.scatter_s(dn_parts.reshape(ns, rows, width)))
            return value
        return after(value, held["one"], ffn_own) if k == nz - 1 else value

    terms, _ = net.scatter_f(weight_part, weight_gate)
    one_sum = held["one"]
    scaled_one = one_sum * gain_one
    grad_input = d_residual + inverse_one * (
        scaled_one - unit_one * jnp.mean(scaled_one * unit_one, axis=-1, keepdims=True)
    )
    term = total_of(terms).astype(BF)
    qkv_own = net.swap_s(term[:, : 3 * cols].reshape(ns, own, 3 * cols))
    grad_query, grad_key, grad_value, grad_attn_gain = unpack_heads(
        qkv_own, attn_gain.astype(F32)[:, None], (w_query, w_key, w_value), ns, nf, per_head
    )
    out_mine = term[:, 3 * cols :].reshape(ns, own, piece).transpose(1, 0, 2).reshape(own, width)
    back_head = [(b, a) for a, b in swap_head]
    grad_out = lax.ppermute(out_mine, BOTH, back_head).astype(F32)
    return (
        layer_out,
        grad_input,
        grad_attn_gain,
        grad_query,
        grad_key,
        grad_value,
        grad_out,
        grad_ffn_gain,
        grad_gate,
        grad_up,
        grad_down,
    )


def solution(mesh):
    row = P(("fsdp", "seq"), None)
    flat = P(("fsdp", "seq"))
    return jax.shard_map(
        shards,
        mesh=mesh,
        in_specs=(row, flat, flat, flat, row, row, row, row, flat, row, row, row, row),
        out_specs=(row, row, flat, row, row, row, row, flat, row, row, row),
        check_vma=False,
    )
```

```python
import functools
import math

import jax
import jax.numpy as jnp
from jax import lax
from jax.experimental import pallas as pl
from jax.experimental.pallas import tpu as pltpu
from jax.sharding import PartitionSpec as P

HEADS = 16
HEAD_DIM = 128
EPSILON = 1e-05
BOTH = ("seq", "fsdp")
BF = jnp.bfloat16
F32 = jnp.float32
TILE = 256
EXTRA = 16
FTILE = 512
VMEM_LIMIT = 56 * 1024 * 1024
PARAMS = pltpu.CompilerParams(vmem_limit_bytes=VMEM_LIMIT)
FFN_PARAMS = pltpu.CompilerParams(vmem_limit_bytes=48 * 1024 * 1024)
WHOLE = pl.BlockSpec(memory_space=pltpu.VMEM)


def nn(left, right):
    return lax.dot_general(left, right, (((1,), (0,)), ((), ())), preferred_element_type=F32)


def nt(left, right):
    return lax.dot_general(left, right, (((1,), (1,)), ((), ())), preferred_element_type=F32)


def tn(left, right):
    return lax.dot_general(left, right, (((0,), (0,)), ((), ())), preferred_element_type=F32)


def after(value, *deps):
    return lax.optimization_barrier((value, *deps))[0]


def shape_of(*dims, dtype=BF):
    return jax.ShapeDtypeStruct(dims, dtype)


def cost(flops, moved):
    return pl.CostEstimate(flops=int(flops), bytes_accessed=int(moved), transcendentals=0)


class Net:
    def __init__(self):
        self.ns = lax.axis_size("seq")
        self.nf = lax.axis_size("fsdp")
        self.nz = self.nf // 2
        ns, nf, nz = self.ns, self.nf, self.nz
        half = ns // 2
        self.s_order = list(range(half)) + list(range(ns - 1, half - 1, -1))
        self.z_order = list(range(0, nz, 2)) + list(range(nz - 1 - nz % 2, 0, -2))
        s_next = {self.s_order[i]: self.s_order[(i + 1) % ns] for i in range(ns)}
        s_prev = {b: a for a, b in s_next.items()}
        z_next = {self.z_order[i]: self.z_order[(i + 1) % nz] for i in range(nz)}
        self.s_perm = [
            (s * nf + f, (s_next[s] if f % 2 == 0 else s_prev[s]) * nf + f)
            for f in range(nf)
            for s in range(ns)
        ]
        self.z_perm = [(2 * z + c, 2 * z_next[z] + c) for z in range(nz) for c in range(2)]
        self.c_perm = [(f, f ^ 1) for f in range(nf)]
        self.f = lax.axis_index("fsdp")
        self.s = lax.axis_index("seq")
        self.c = self.f % 2
        self.z = self.f // 2
        self.s_place = self.fold(self.s)
        self.z_place = jnp.where(self.z % 2 == 0, self.z // 2, nz - 1 - self.z // 2)
        self.s_sign = 1 - 2 * self.c

    def fold(self, value):
        half = self.ns // 2
        return jnp.where(value < half, value, self.ns - 1 + half - value)

    def s_back(self, k):
        return self.fold((self.s_place - self.s_sign * k + self.ns) % self.ns)

    def z_back(self, k):
        place = (self.z_place - k + self.nz) % self.nz
        return jnp.where(2 * place < self.nz, 2 * place, 2 * (self.nz - 1 - place) + 1)

    def step_s(self, value):
        return lax.ppermute(value, BOTH, self.s_perm)

    def step_z(self, value):
        return lax.ppermute(value, "fsdp", self.z_perm)

    def swap_c(self, value):
        return lax.ppermute(value, "fsdp", self.c_perm)

    def ring_s(self, value):
        blocks = [value]
        for _ in range(1, self.ns):
            blocks.append(self.step_s(blocks[-1]))
        return blocks

    def ring_f(self, value, gate=lambda k, value: value):
        held, blocks = value, []
        for k in range(self.nz):
            if k:
                held = self.step_z(gate(k, held))
            blocks += [held, self.swap_c(held)]
        return blocks

    def origin_f(self):
        out = []
        for k in range(self.nz):
            out += [self.z_back(k) * 2 + self.c, self.z_back(k) * 2 + 1 - self.c]
        return jnp.stack(out).astype(jnp.int32)

    def swap_s(self, blocks):
        out = blocks
        for k in range(1, self.ns):
            perm = [(s, s ^ k) for s in range(self.ns)]
            piece = lax.dynamic_index_in_dim(blocks, self.s ^ k, 0, keepdims=True)
            got = lax.ppermute(piece, "seq", perm)
            out = lax.dynamic_update_slice_in_dim(out, got, self.s ^ k, 0)
        return out

    def natural_s(self, blocks):
        out = jnp.zeros((self.ns, *blocks[0].shape), blocks[0].dtype)
        for k, block in enumerate(blocks):
            out = lax.dynamic_update_slice_in_dim(out, block[None], self.s_back(k), 0)
        return out

    def scatter_s(self, parts, gate=lambda k, value: value):
        came = None
        for k in range(1, self.ns):
            total = parts[k] if came is None else parts[k].astype(F32) + came.astype(F32)
            came = self.step_s(gate(k, total.astype(BF)))
        return parts[0], came

    def scatter_f(self, part, gate=lambda k, value, sent: value):
        came, sent = None, []
        for k in range(1, self.nz + 1):
            mine, away = part(k % self.nz, sent)
            other = self.swap_c(away)
            if k == self.nz:
                return (mine, other, came), sent
            total = mine.astype(F32) + other.astype(F32)
            if came is not None:
                total = total + came.astype(F32)
            sent.append(gate(k, total.astype(BF), sent))
            came = self.step_z(sent[-1])


def split(values, count):
    return tuple(values[:count]), list(values[count:])


def total_of(terms):
    return sum(term.astype(F32) for term in terms)


def pack_ffn_kernel(fcols, gate_ref, up_ref, out_ref):
    for i in range(gate_ref.shape[1] // fcols):
        for t in range(fcols // FTILE):
            here = slice(i * fcols + t * FTILE, i * fcols + (t + 1) * FTILE)
            out_ref[i, :, 2 * t * FTILE : (2 * t + 1) * FTILE] = gate_ref[:, here]
            out_ref[i, :, (2 * t + 1) * FTILE : (2 * t + 2) * FTILE] = up_ref[:, here]


def pack_ffn(w_gate, w_up, nf):
    own, hidden = w_gate.shape
    fcols = hidden // nf
    return pl.pallas_call(
        functools.partial(pack_ffn_kernel, fcols),
        grid=(nf // 2,),
        in_specs=[pl.BlockSpec((own, 2 * fcols), lambda i: (0, i))] * 2,
        out_specs=pl.BlockSpec((2, own, 2 * fcols), lambda i: (i, 0, 0)),
        out_shape=shape_of(nf, own, 2 * fcols),
    )(w_gate, w_up)


def unpack_ffn_kernel(fcols, w_gate_ref, w_up_ref, gain_ref, in_ref, *out_refs):
    gate_ref, up_ref, gain_out_ref = out_refs
    total = jnp.zeros(gain_out_ref.shape, F32)
    for t in range(fcols // FTILE):
        here = slice(t * FTILE, (t + 1) * FTILE)
        gate = in_ref[0, :, 2 * t * FTILE : (2 * t + 1) * FTILE].astype(F32)
        upward = in_ref[0, :, (2 * t + 1) * FTILE : (2 * t + 2) * FTILE].astype(F32)
        gate_ref[:, here] = gate
        up_ref[:, here] = upward
        both = gate * w_gate_ref[:, here].astype(F32) + upward * w_up_ref[:, here].astype(F32)
        total = total + jnp.sum(both, axis=1, keepdims=True)

    @pl.when(pl.program_id(0) == 0)
    def _():
        gain_out_ref[...] = jnp.zeros_like(gain_out_ref)

    gain_out_ref[...] += total / gain_ref[...]


def unpack_ffn(w_gate, w_up, gain, blocks):
    own, hidden = w_gate.shape
    nf = blocks.shape[0]
    fcols = hidden // nf
    wide = pl.BlockSpec((own, fcols), lambda i: (0, i))
    thin = pl.BlockSpec((own, 1), lambda i: (0, 0))
    gate, upward, grad_gain = pl.pallas_call(
        functools.partial(unpack_ffn_kernel, fcols),
        grid=(nf,),
        in_specs=[wide, wide, thin, pl.BlockSpec((1, own, 2 * fcols), lambda i: (i, 0, 0))],
        out_specs=[wide, wide, thin],
        out_shape=[
            shape_of(own, hidden, dtype=F32),
            shape_of(own, hidden, dtype=F32),
            shape_of(own, 1, dtype=F32),
        ],
    )(w_gate, w_up, gain, blocks)
    return gate, upward, grad_gain[:, 0]


def head_of(s, j, ns, nf, per_head):
    sh, fl = divmod(s, per_head)
    return (j * per_head + fl) * (ns // per_head) + sh


def pack_heads_kernel(ns, nf, per_head, *refs):
    *in_refs, extra_ref, out_ref = refs
    heads = HEADS // ns
    own = in_refs[0].shape[0]
    for s in range(ns):
        out_ref[s, own:, :] = jnp.zeros((EXTRA, out_ref.shape[2]), BF)
        out_ref[s, own:, : extra_ref.shape[1]] = extra_ref[...]
        for i, ref in enumerate(in_refs):
            for j in range(heads):
                h = head_of(s, j, ns, nf, per_head)
                at = (i * heads + j) * HEAD_DIM
                out_ref[s, :own, at : at + HEAD_DIM] = ref[:, h * HEAD_DIM : (h + 1) * HEAD_DIM]


def pack_heads(weights, extra, ns, nf, per_head):
    own, width = weights[0].shape
    return pl.pallas_call(
        functools.partial(pack_heads_kernel, ns, nf, per_head),
        in_specs=[WHOLE] * 4,
        out_specs=WHOLE,
        out_shape=shape_of(ns, own + EXTRA, 3 * width // ns),
        compiler_params=PARAMS,
    )(*weights, extra)


def unpack_heads_kernel(ns, nf, per_head, in_ref, gain_ref, *refs):
    weight_refs, grad_refs, gain_out_ref = refs[:3], refs[3:6], refs[6]
    heads = HEADS // ns
    total = jnp.zeros(gain_out_ref.shape, F32)
    for s in range(ns):
        for i in range(3):
            for j in range(heads):
                h = head_of(s, j, ns, nf, per_head)
                at = (i * heads + j) * HEAD_DIM
                here = slice(h * HEAD_DIM, (h + 1) * HEAD_DIM)
                grad = in_ref[s, :, at : at + HEAD_DIM].astype(F32)
                grad_refs[i][:, here] = grad
                total = total + jnp.sum(
                    grad * weight_refs[i][:, here].astype(F32), axis=1, keepdims=True
                )
    gain_out_ref[...] = total / gain_ref[...]


def unpack_heads(blocks, gain, weights, ns, nf, per_head):
    own, width = weights[0].shape
    *grads, grad_gain = pl.pallas_call(
        functools.partial(unpack_heads_kernel, ns, nf, per_head),
        in_specs=[WHOLE] * 5,
        out_specs=[WHOLE] * 4,
        out_shape=[shape_of(own, width, dtype=F32)] * 3 + [shape_of(own, 1, dtype=F32)],
        compiler_params=PARAMS,
    )(blocks, gain, *weights)
    return *grads, grad_gain[:, 0]


def spin(field, cosine, sine):
    return field * cosine + pltpu.roll(field, HEAD_DIM // 2, 1) * sine


def lay_out_weight(origin_ref, blocks, start, own, ns, out_ref):
    piece = out_ref.shape[1] // ns
    for j, block in enumerate(blocks):
        row = pl.multiple_of(origin_ref[j] * own, own)
        for q in range(ns):
            out_ref[pl.ds(row, own), q * piece : (q + 1) * piece] = block[
                q * own : (q + 1) * own, start:
            ]


def weights_of(scores, scale, bias, mask):
    return jnp.where(mask, jax.nn.sigmoid(scores * scale + bias), 0.0)


def mask_of(col_ref, row_ref):
    return (row_ref[0:1, :] <= col_ref[:, 0:1]) & (row_ref[1:2, :] == col_ref[:, 1:2])


def attend_kernel(
    dims, origin_ref, input_ref, inverse_ref, cos_ref, sin_ref, col_ref, row_ref, *refs
):
    ns, nf, own, cols, scale, bias = dims
    blocks = refs[:nf]
    q_ref, k_ref, v_ref, mixed_ref, att_ref, normed_ref, gains_ref, out_w = refs[nf:]
    deep = ns * own
    lay_out_weight(origin_ref, blocks, 3 * cols, own, ns, out_w)
    for j, block in enumerate(blocks):
        here = pl.ds(pl.multiple_of(origin_ref[j] * deep, deep), deep)
        gains = block[deep : deep + EXTRA, :deep].astype(F32)
        gains_ref[:, here] = gains
        unit = input_ref[:, here].astype(F32) * inverse_ref[...]
        normed_ref[:, here] = (unit * gains[0:1, :]).astype(BF)
    for part, ref in enumerate((q_ref, k_ref, v_ref)):

        @pl.loop(0, cols // TILE)
        def _(t, part=part, ref=ref):
            at = pl.multiple_of(part * cols + t * TILE, TILE)
            total = None
            for j, block in enumerate(blocks):
                from_col = pl.multiple_of(origin_ref[j] * deep, deep)
                term = nn(normed_ref[:, pl.ds(from_col, deep)], block[:deep, pl.ds(at, TILE)])
                total = term if total is None else total + term
            for i in range(TILE // HEAD_DIM):
                field = total[:, i * HEAD_DIM : (i + 1) * HEAD_DIM]
                if part < 2:
                    field = spin(field, cos_ref[...], sin_ref[...])
                to = pl.multiple_of(t * TILE + i * HEAD_DIM, HEAD_DIM)
                ref[:, pl.ds(to, HEAD_DIM)] = field.astype(BF)

    mask = mask_of(col_ref, row_ref)

    @pl.loop(0, cols // HEAD_DIM)
    def _(h):
        here = pl.ds(pl.multiple_of(h * HEAD_DIM, HEAD_DIM), HEAD_DIM)
        weights = weights_of(nt(q_ref[:, here], k_ref[:, here]), scale, bias, mask)
        mixed_ref[:, here] = nn(weights.astype(BF), v_ref[:, here]).astype(BF)

    wide = 512

    @pl.loop(0, att_ref.shape[1] // wide)
    def _(t):
        here = pl.ds(pl.multiple_of(t * wide, wide), wide)
        att_ref[:, here] = nn(mixed_ref[...], out_w[:, here]).astype(BF)


def attend(dims, origin, rows, inverse, tables, marks, blocks):
    ns, nf, own, cols, _, _ = dims
    group, width = rows.shape
    small = shape_of(group, cols)
    return pl.pallas_call(
        functools.partial(attend_kernel, dims),
        in_specs=[pl.BlockSpec(memory_space=pltpu.SMEM)] + [WHOLE] * (6 + nf),
        out_specs=[WHOLE] * 7,
        out_shape=[small] * 4
        + [shape_of(group, width)] * 2
        + [shape_of(EXTRA, width, dtype=F32)],
        scratch_shapes=[pltpu.VMEM((cols, width), BF)],
        compiler_params=PARAMS,
        cost_estimate=cost(
            2 * group * width * cols * 4 + 4 * group * group * cols, 2 * width * cols * 4
        ),
    )(origin, rows, inverse, *tables, *marks, *blocks)


def attend_back_kernel(
    dims, origin_ref, datt_ref, q_ref, k_ref, v_ref, mixed_ref, cos_ref, sin_ref, col_ref, row_ref,
    *refs
):
    ns, nf, own, cols, scale, bias = dims
    blocks = refs[:nf]
    d_qkv, out_term, out_w = refs[nf:]
    piece = datt_ref.shape[1] // ns
    lay_out_weight(origin_ref, blocks, 0, own, ns, out_w)
    mask = mask_of(col_ref, row_ref)

    @pl.loop(0, cols // HEAD_DIM)
    def _(h):
        start = pl.multiple_of(h * HEAD_DIM, HEAD_DIM)
        here = pl.ds(start, HEAD_DIM)
        query, key = q_ref[:, here], k_ref[:, here]
        d_mixed = nt(datt_ref[...], out_w[here, :]).astype(BF)
        weights = weights_of(nt(query, key), scale, bias, mask)
        d_weights = nt(d_mixed, v_ref[:, here])
        d_scores = (d_weights * weights * (1.0 - weights)).astype(BF)
        d_query = nn(d_scores, key) * scale
        d_key = tn(d_scores, query) * scale
        d_value = tn(weights.astype(BF), d_mixed)
        d_qkv[:, here] = spin(d_query, cos_ref[...], -sin_ref[...]).astype(BF)
        d_qkv[:, pl.ds(pl.multiple_of(cols + start, HEAD_DIM), HEAD_DIM)] = spin(
            d_key, cos_ref[...], -sin_ref[...]
        ).astype(BF)
        d_qkv[:, pl.ds(pl.multiple_of(2 * cols + start, HEAD_DIM), HEAD_DIM)] = d_value.astype(BF)

    @pl.loop(0, ns)
    def _(q):
        here = pl.ds(pl.multiple_of(q * piece, piece), piece)
        out_term[q] = tn(mixed_ref[...], datt_ref[:, here]).astype(BF)


def attend_back(dims, origin, datt, saved, tables, marks, blocks):
    ns, nf, own, cols, _, _ = dims
    group, width = datt.shape
    piece = width // ns
    last = pl.BlockSpec((ns * own, piece), lambda i: (0, 3 * cols // piece))

    def full(*shape):
        return pl.BlockSpec(shape, lambda i: (0,) * len(shape))

    arrays = [datt, *saved, *tables, *marks]
    return pl.pallas_call(
        functools.partial(attend_back_kernel, dims),
        grid=(1,),
        in_specs=[pl.BlockSpec(memory_space=pltpu.SMEM)]
        + [full(*array.shape) for array in arrays]
        + [last] * nf,
        out_specs=[full(group, 3 * cols), full(ns, cols, piece)],
        out_shape=[shape_of(group, 3 * cols), shape_of(ns, cols, piece)],
        scratch_shapes=[pltpu.VMEM((cols, width), BF)],
        compiler_params=PARAMS,
        cost_estimate=cost(
            2 * group * width * cols * 2 + 10 * group * group * cols, 4 * width * cols
        ),
    )(origin, *arrays, *blocks)


def weight_grad_kernel(dims, step, origin_ref, normed_ref, d_ref, out_ref, mine_ref, away_ref):
    ns, nf, own, cols, _, _ = dims
    deep = ns * own
    for i, ref in enumerate((mine_ref, away_ref)):
        origin = origin_ref[2 * step + i]
        here = pl.ds(pl.multiple_of(origin * deep, deep), deep)
        ref[:, : 3 * cols] = tn(normed_ref[:, here], d_ref[...]).astype(BF)
        row = pl.multiple_of(origin * own, own)
        for q in range(ns):
            ref[q * own : (q + 1) * own, 3 * cols :] = out_ref[q, pl.ds(row, own), :]


def weight_grad(dims, step, origin, normed, d_qkv, out_term):
    ns, nf, own, cols, _, _ = dims
    term = shape_of(ns * own, 3 * cols + out_term.shape[2])
    return pl.pallas_call(
        functools.partial(weight_grad_kernel, dims, step),
        in_specs=[pl.BlockSpec(memory_space=pltpu.SMEM)] + [WHOLE] * 3,
        out_specs=[WHOLE] * 2,
        out_shape=[term, term],
        compiler_params=PARAMS,
        cost_estimate=cost(12 * normed.shape[0] * ns * own * cols, 2**23),
    )(origin, normed, d_qkv, out_term)


def input_grad_kernel(dims, origin_ref, d_ref, *refs):
    ns, nf, own, cols, _, _ = dims
    *blocks, dn_ref = refs
    deep = ns * own
    for j, block in enumerate(blocks):
        here = pl.ds(pl.multiple_of(origin_ref[j] * deep, deep), deep)
        dn_ref[:, here] = nt(d_ref[...], block[:deep, : 3 * cols]).astype(BF)


def input_grad(dims, origin, d_qkv, blocks, width):
    ns, nf, own, cols, _, _ = dims
    group = d_qkv.shape[0]
    return pl.pallas_call(
        functools.partial(input_grad_kernel, dims),
        in_specs=[pl.BlockSpec(memory_space=pltpu.SMEM)] + [WHOLE] * (1 + nf),
        out_specs=WHOLE,
        out_shape=shape_of(group, width),
        compiler_params=PARAMS,
        cost_estimate=cost(6 * group * width * cols, 8 * width * cols),
    )(origin, d_qkv, *blocks)


def ffn_kernel(count, first, *refs):
    unit_refs, cot_refs, refs = refs[:count], refs[count : 2 * count], refs[2 * count :]
    weight_ref, down_ref = refs[:2]
    refs = refs[2 if first else 6 :]
    inner_ref, d_ref, unit_ref, cot_ref = refs[:4]
    two_refs, out_refs, two, out = refs[4 : 4 + count], refs[4 + count : 4 + 2 * count], *refs[-2:]
    rows = unit_refs[0].shape[0]
    j = pl.program_id(0)

    @pl.when(j == 0)
    def _():
        for i in range(count):
            unit_ref[i * rows : (i + 1) * rows, :] = unit_refs[i][...]
            cot_ref[i * rows : (i + 1) * rows, :] = cot_refs[i][...]

    both = nn(unit_ref[...], weight_ref[...])
    d_inner = nt(cot_ref[...], down_ref[...])
    gate, upward = both[:, :FTILE], both[:, FTILE:]
    sigma = jax.nn.sigmoid(gate)
    silu = gate * sigma
    inner_ref[...] = (silu * upward).astype(BF)
    d_ref[:, :FTILE] = (d_inner * upward * sigma * (1.0 + gate * (1.0 - sigma))).astype(BF)
    d_ref[:, FTILE:] = (d_inner * silu).astype(BF)
    two_term = nt(d_ref[...], weight_ref[...])
    out_term = nn(inner_ref[...], down_ref[...])

    @pl.when(j == 0)
    def _():
        two[...] = two_term
        out[...] = out_term

    @pl.when(j > 0)
    def _():
        two[...] += two_term
        out[...] += out_term

    @pl.when(j == pl.num_programs(0) - 1)
    def _():
        for i in range(count):
            two_refs[i][...] = two[i * rows : (i + 1) * rows, :].astype(BF)
            out_refs[i][...] = out[i * rows : (i + 1) * rows, :].astype(BF)


def ffn(turn, turns, units, cots, weight, down, before):
    rows, width = units[0].shape
    count = len(units)
    fcols = down.shape[0]
    all_rows = count * rows
    whole = pl.BlockSpec((rows, width), lambda j: (0, 0))
    shared = [
        ((all_rows, FTILE), lambda j: (turn, j), fcols),
        ((all_rows, 2 * FTILE), lambda j: (turn, j), 2 * fcols),
        ((all_rows, width), lambda j: (turn, 0), width),
        ((all_rows, width), lambda j: (turn, 0), width),
    ]
    return pl.pallas_call(
        functools.partial(ffn_kernel, count, not before),
        grid=(fcols // FTILE,),
        in_specs=[whole] * (2 * count)
        + [
            pl.BlockSpec((width, 2 * FTILE), lambda j: (0, j)),
            pl.BlockSpec((FTILE, width), lambda j: (j, 0)),
        ]
        + [pl.BlockSpec(memory_space=pl.ANY)] * len(before),
        out_specs=[pl.BlockSpec(shape, at) for shape, at, _ in shared] + [whole] * (2 * count),
        out_shape=[shape_of(turns * all_rows, last) for _, _, last in shared]
        + [shape_of(rows, width)] * (2 * count),
        scratch_shapes=[pltpu.VMEM((all_rows, width), F32)] * 2,
        input_output_aliases={2 * count + 2 + i: i for i in range(len(before))},
        compiler_params=FFN_PARAMS,
        cost_estimate=cost(
            12 * all_rows * width * fcols, 2 * (3 * fcols + 4 * all_rows) * width
        ),
    )(*units, *cots, weight, down, *before)


def norm_two_kernel(ns, nf, own, input_ref, part_ref, came_ref, gain_ref, *out_refs):
    residual_ref, inverse_ref, unit_ref = out_refs
    residual = (
        input_ref[...].astype(F32) + part_ref[...].astype(F32) + came_ref[...].astype(F32)
    )
    inverse = lax.rsqrt(jnp.mean(residual * residual, axis=-1, keepdims=True) + EPSILON)
    residual_ref[...] = residual
    inverse_ref[...] = inverse
    normed = (residual * inverse * gain_ref[...]).astype(BF)
    for f in range(nf):
        for s in range(ns):
            here, there = (f * ns + s) * own, (s * nf + f) * own
            unit_ref[:, there : there + own] = normed[:, here : here + own]


def norm_two(ns, nf, own, rows, part, came, gain):
    count, width = rows.shape
    return pl.pallas_call(
        functools.partial(norm_two_kernel, ns, nf, own),
        in_specs=[WHOLE] * 4,
        out_specs=[WHOLE] * 3,
        out_shape=[
            shape_of(count, width, dtype=F32),
            shape_of(count, 1, dtype=F32),
            shape_of(count, width),
        ],
        compiler_params=PARAMS,
    )(rows, part, came, gain)


def norm_two_back_kernel(ns, nf, own, *refs):
    term_refs, (residual_ref, inverse_ref, gain_ref, cot_ref) = refs[:3], refs[3:7]
    d_ref, low_ref, scaled = refs[7:]
    total = term_refs[0][...].astype(F32)
    for ref in term_refs[1:]:
        total = total + ref[...].astype(F32)
    for f in range(nf):
        for s in range(ns):
            here, there = (f * ns + s) * own, (s * nf + f) * own
            scaled[:, here : here + own] = total[:, there : there + own]
    unit = residual_ref[...] * inverse_ref[...]
    back = scaled[...] * gain_ref[...]
    mean = jnp.mean(back * unit, axis=-1, keepdims=True)
    d_residual = cot_ref[...].astype(F32) + inverse_ref[...] * (back - unit * mean)
    d_ref[...] = d_residual
    low_ref[...] = d_residual.astype(BF)


def norm_two_back(ns, nf, own, terms, residual, inverse, gain, cot):
    count, width = residual.shape
    return pl.pallas_call(
        functools.partial(norm_two_back_kernel, ns, nf, own),
        in_specs=[WHOLE] * 7,
        out_specs=[WHOLE] * 2,
        out_shape=[shape_of(count, width, dtype=F32), shape_of(count, width)],
        scratch_shapes=[pltpu.VMEM((count, width), F32)],
        compiler_params=PARAMS,
    )(*terms, residual, inverse, gain, cot)


def shards(
    inputs,
    positions,
    seq_ids,
    attn_gain,
    w_query,
    w_key,
    w_value,
    w_out,
    ffn_gain,
    w_gate,
    w_up,
    w_down,
    cotangent,
):
    net = Net()
    ns, nf, nz = net.ns, net.nf, net.nz
    rows, width = inputs.shape
    group = rows * ns
    own = w_query.shape[0]
    hidden = w_gate.shape[1]
    fcols = hidden // nf
    per_head = HEAD_DIM // own
    swap_head = []
    for f in range(nf):
        for s in range(ns):
            fh, fl = divmod(f, per_head)
            sh, sl = divmod(s, per_head)
            swap_head.append((s * nf + f, (sh * per_head + fl) * nf + fh * per_head + sl))
    cols = HEADS // ns * HEAD_DIM
    piece = width // ns
    dims = (ns, nf, own, cols, HEAD_DIM ** (-0.5), -math.log(group))

    origin = net.origin_f()
    extra = jnp.stack(
        [
            (positions // 256).astype(BF),
            (positions % 256).astype(BF),
            seq_ids.astype(BF),
            jnp.pad(jnp.concatenate([attn_gain, ffn_gain]), (0, rows - 2 * own)),
        ]
    )
    extra = jnp.pad(extra, ((0, EXTRA - 4), (0, 0)))

    down_all = lax.all_gather(w_down, "seq", axis=0, tiled=True)
    packed_ffn = pack_ffn(w_gate, w_up, nf)
    ffn_rows = lax.all_to_all(packed_ffn, "fsdp", split_axis=0, concat_axis=0, tiled=True)
    packed = pack_heads((w_query, w_key, after(w_value, packed_ffn)), extra, ns, nf, per_head)
    qkv_rows = net.swap_s(packed)
    out_rows = lax.ppermute(w_out, BOTH, swap_head)
    input_ring = net.ring_s(inputs)
    marks = qkv_rows[:, own : own + 4, :rows].astype(F32)
    gain_rows = marks[:, 3, : 2 * own].reshape(ns, 2, own).transpose(1, 0, 2).reshape(2, ns * own)
    merged = jnp.concatenate(
        [
            qkv_rows[:, :own].reshape(ns * own, 3 * cols),
            out_rows.reshape(own, ns, piece).transpose(1, 0, 2).reshape(ns * own, piece),
        ],
        axis=1,
    )
    merged = jnp.concatenate(
        [
            merged,
            jnp.pad(gain_rows.astype(BF), ((0, EXTRA - 2), (0, 3 * cols + piece - ns * own))),
        ],
        axis=0,
    )
    blocks = net.ring_f(merged)
    w_ffn = lax.all_gather(
        after(ffn_rows, blocks[2]).reshape(nf * own, 2 * fcols), "seq", axis=0, tiled=True
    )

    input_all = jnp.concatenate(input_ring, axis=0)
    squares = jnp.mean(jnp.square(input_all.astype(F32)), axis=-1, keepdims=True)
    inverse_all = lax.rsqrt(squares + EPSILON)
    input_float = inputs.astype(F32)
    inverse_one = inverse_all[:rows]
    unit_one = input_float * inverse_one
    order = [net.s_back(k) for k in range(ns)]
    marks = jnp.stack([lax.dynamic_index_in_dim(marks, s, 0, keepdims=False) for s in order])
    places = (marks[:, 0] * 256.0 + marks[:, 1]).reshape(group)
    ids = marks[:, 2].reshape(group)
    index = jnp.concatenate([(s * rows + jnp.arange(rows)).astype(F32) for s in order])
    frequency = 10000.0 ** (-(jnp.arange(HEAD_DIM // 2, dtype=F32) * 2.0) / HEAD_DIM)
    angles = places[:, None] * frequency[None, :]
    cosine, sine = jnp.cos(angles), jnp.sin(angles)
    tables = (
        jnp.concatenate([cosine, cosine], axis=1),
        jnp.concatenate([-sine, sine], axis=1),
    )
    row_marks = jnp.stack([index, ids])
    pair_marks = (row_marks.T, row_marks)

    *saved, attended, normed_all, gains = attend(
        dims, origin, input_all, inverse_all, tables, pair_marks, blocks
    )
    gain_one, gain_two = gains[0:1], gains[1:2]
    cots = net.ring_f(after(cotangent, blocks[-2]))
    att_terms = net.scatter_s(
        attended.reshape(ns, rows, width),
        lambda k, value: after(value, cots[2 * k]) if k < nz else value,
    )

    residual, inverse_two, unit_low = norm_two(ns, nf, own, inputs, *att_terms, gain_two)
    unit_two = residual * inverse_two
    turns = 2 if nz % 2 == 0 else 1
    each = 2 * nz // turns
    shared, two_parts, out_parts = (), [], []
    units = []

    def run_turn(turn, ready):
        nonlocal shared
        here = slice(each * turn, each * (turn + 1))
        shared, done = split(
            ffn(turn, turns, units_at(here, ready), cots[here], w_ffn, down_all, shared), 4
        )
        two_parts.extend(done[:each])
        out_parts.extend(done[each:])

    def units_at(here, ready):
        return units[here] if ready is None else after(units[here], ready)

    held_unit = unit_low
    for k in range(nz):
        if k:
            held_unit = net.step_z(
                after(held_unit, two_parts[0]) if k == each // 2 + 1 else held_unit
            )
        units += [held_unit, net.swap_c(held_unit)]
        if 2 * k + 2 == each:
            run_turn(0, None)
    sums = {}

    def two_part(k, sent):
        if 2 * k + 2 > len(two_parts):
            run_turn(1, sent[0])
        return two_parts[2 * k : 2 * k + 2]

    def two_gate(k, value, sent):
        if k == nz - 1:
            inner, d_ffn, unit_all, cot_all = shared
            sums["down"] = tn(after(inner, sent[-1]), cot_all).astype(BF)
            return after(value, sums["down"])
        return value

    two_terms, two_sent = net.scatter_f(two_part, two_gate)
    inner, d_ffn, unit_all, cot_all = shared
    grad_down = lax.psum_scatter(
        sums["down"], "seq", scatter_dimension=0, tiled=True
    ).astype(F32)
    sums["ffn"] = tn(after(unit_all, two_sent[-1]), d_ffn).astype(BF)
    two_terms = (after(two_terms[0], sums["ffn"]), *two_terms[1:])
    d_residual, d_low = norm_two_back(
        ns, nf, own, two_terms, residual, inverse_two, gain_two, cotangent
    )
    d_attended, out_came = [d_low], [None]

    def send_out(k, ready):
        other = net.swap_c(out_parts[2 * k + 1])
        total = out_parts[2 * k].astype(F32) + other.astype(F32)
        if k > 1:
            total = total + out_came[-1].astype(F32)
        out_came.append(net.step_z(after(total.astype(BF), ready)))

    for k in range(1, ns):
        value = d_attended[-1]
        d_attended.append(net.step_s(after(value, out_came[1]) if k == ns - 1 else value))
        if k == 1:
            send_out(1, d_attended[1])
    ffn_sum = lax.psum_scatter(
        after(sums["ffn"], d_attended[-1]).reshape(ns, nf * own, 2 * fcols),
        "seq",
        scatter_dimension=0,
        tiled=False,
    )
    for k in range(2, nz):
        send_out(k, d_low)
    out_terms = (out_parts[0], net.swap_c(out_parts[1]), out_came[-1])
    layer_out = (residual + total_of(out_terms)).astype(BF)
    ffn_own = lax.all_to_all(
        ffn_sum.reshape(nf, own, 2 * fcols), "fsdp", split_axis=0, concat_axis=0, tiled=True
    )
    grad_gate, grad_up, grad_ffn_gain = unpack_ffn(
        w_gate,
        w_up,
        ffn_gain.astype(F32)[:, None],
        ffn_own,
    )

    d_qkv, out_grad = attend_back(
        dims, origin, jnp.concatenate(d_attended, axis=0), saved, tables, pair_marks, blocks
    )
    held = {}

    def weight_part(k, sent):
        if k == 1:
            ready = after(d_qkv, out_came[-2])
        else:
            ready = after(d_qkv, sent[min(len(sent), 2) - 1])
        return weight_grad(dims, k, origin, normed_all, ready, out_grad)

    def weight_gate(k, value, sent):
        if k == 2:
            dn_parts = input_grad(dims, origin, after(d_qkv, sent[0]), blocks, width)
            held["one"] = total_of(net.scatter_s(dn_parts.reshape(ns, rows, width)))
            return after(value, out_terms[2])
        return after(value, held["one"]) if k == nz - 1 else value

    terms, _ = net.scatter_f(weight_part, weight_gate)
    one_sum = held["one"]
    scaled_one = one_sum * gain_one
    grad_input = d_residual + inverse_one * (
        scaled_one - unit_one * jnp.mean(scaled_one * unit_one, axis=-1, keepdims=True)
    )
    term = total_of(terms).astype(BF)
    qkv_own = net.swap_s(term[:, : 3 * cols].reshape(ns, own, 3 * cols))
    grad_query, grad_key, grad_value, grad_attn_gain = unpack_heads(
        qkv_own, attn_gain.astype(F32)[:, None], (w_query, w_key, w_value), ns, nf, per_head
    )
    out_mine = term[:, 3 * cols :].reshape(ns, own, piece).transpose(1, 0, 2).reshape(own, width)
    back_head = [(b, a) for a, b in swap_head]
    grad_out = lax.ppermute(out_mine, BOTH, back_head).astype(F32)
    return (
        layer_out,
        grad_input,
        grad_attn_gain,
        grad_query,
        grad_key,
        grad_value,
        grad_out,
        grad_ffn_gain,
        grad_gate,
        grad_up,
        grad_down,
    )


def solution(mesh):
    row = P(("fsdp", "seq"), None)
    flat = P(("fsdp", "seq"))
    return jax.shard_map(
        shards,
        mesh=mesh,
        in_specs=(row, flat, flat, flat, row, row, row, row, flat, row, row, row, row),
        out_specs=(row, row, flat, row, row, row, row, flat, row, row, row),
        check_vma=False,
    )
```

```python
import functools
import math

import jax
import jax.numpy as jnp
from jax import lax
from jax.experimental import pallas as pl
from jax.experimental.pallas import tpu as pltpu
from jax.sharding import PartitionSpec as P

HEADS = 16
HEAD_DIM = 128
EPSILON = 1e-05
BOTH = ("seq", "fsdp")
BF = jnp.bfloat16
F32 = jnp.float32
TILE = 256
EXTRA = 16
FTILE = 512
VMEM_LIMIT = 32 * 1024 * 1024
PARAMS = pltpu.CompilerParams(vmem_limit_bytes=VMEM_LIMIT)
FFN_PARAMS = pltpu.CompilerParams(vmem_limit_bytes=48 * 1024 * 1024)
WHOLE = pl.BlockSpec(memory_space=pltpu.VMEM)


def nn(left, right):
    return lax.dot_general(left, right, (((1,), (0,)), ((), ())), preferred_element_type=F32)


def nt(left, right):
    return lax.dot_general(left, right, (((1,), (1,)), ((), ())), preferred_element_type=F32)


def tn(left, right):
    return lax.dot_general(left, right, (((0,), (0,)), ((), ())), preferred_element_type=F32)


def after(value, *deps):
    return lax.optimization_barrier((value, *deps))[0]


def shape_of(*dims, dtype=BF):
    return jax.ShapeDtypeStruct(dims, dtype)


def cost(flops, moved):
    return pl.CostEstimate(flops=int(flops), bytes_accessed=int(moved), transcendentals=0)


class Net:
    def __init__(self):
        self.ns = lax.axis_size("seq")
        self.nf = lax.axis_size("fsdp")
        self.nz = self.nf // 2
        ns, nf, nz = self.ns, self.nf, self.nz
        half = ns // 2
        self.s_order = list(range(half)) + list(range(ns - 1, half - 1, -1))
        self.z_order = list(range(0, nz, 2)) + list(range(nz - 1 - nz % 2, 0, -2))
        s_next = {self.s_order[i]: self.s_order[(i + 1) % ns] for i in range(ns)}
        s_prev = {b: a for a, b in s_next.items()}
        z_next = {self.z_order[i]: self.z_order[(i + 1) % nz] for i in range(nz)}
        self.s_perm = [
            (s * nf + f, (s_next[s] if f % 2 == 0 else s_prev[s]) * nf + f)
            for f in range(nf)
            for s in range(ns)
        ]
        self.z_perm = [(2 * z + c, 2 * z_next[z] + c) for z in range(nz) for c in range(2)]
        self.c_perm = [(f, f ^ 1) for f in range(nf)]
        self.f = lax.axis_index("fsdp")
        self.s = lax.axis_index("seq")
        self.c = self.f % 2
        self.z = self.f // 2
        self.s_place = self.fold(self.s)
        self.z_place = jnp.where(self.z % 2 == 0, self.z // 2, nz - 1 - self.z // 2)
        self.s_sign = 1 - 2 * self.c

    def fold(self, value):
        half = self.ns // 2
        return jnp.where(value < half, value, self.ns - 1 + half - value)

    def s_back(self, k):
        return self.fold((self.s_place - self.s_sign * k + self.ns) % self.ns)

    def z_back(self, k):
        place = (self.z_place - k + self.nz) % self.nz
        return jnp.where(2 * place < self.nz, 2 * place, 2 * (self.nz - 1 - place) + 1)

    def step_s(self, value):
        return lax.ppermute(value, BOTH, self.s_perm)

    def step_z(self, value):
        return lax.ppermute(value, "fsdp", self.z_perm)

    def swap_c(self, value):
        return lax.ppermute(value, "fsdp", self.c_perm)

    def ring_s(self, value):
        blocks = [value]
        for _ in range(1, self.ns):
            blocks.append(self.step_s(blocks[-1]))
        return blocks

    def ring_f(self, value, gate=lambda k, value: value):
        held, blocks = value, []
        for k in range(self.nz):
            if k:
                held = self.step_z(gate(k, held))
            blocks += [held, self.swap_c(held)]
        return blocks

    def origin_f(self):
        out = []
        for k in range(self.nz):
            out += [self.z_back(k) * 2 + self.c, self.z_back(k) * 2 + 1 - self.c]
        return jnp.stack(out).astype(jnp.int32)

    def swap_s(self, blocks):
        out = blocks
        for k in range(1, self.ns):
            perm = [(s, s ^ k) for s in range(self.ns)]
            piece = lax.dynamic_index_in_dim(blocks, self.s ^ k, 0, keepdims=True)
            got = lax.ppermute(piece, "seq", perm)
            out = lax.dynamic_update_slice_in_dim(out, got, self.s ^ k, 0)
        return out

    def natural_s(self, blocks):
        out = jnp.zeros((self.ns, *blocks[0].shape), blocks[0].dtype)
        for k, block in enumerate(blocks):
            out = lax.dynamic_update_slice_in_dim(out, block[None], self.s_back(k), 0)
        return out

    def scatter_s(self, parts, gate=lambda k, value: value):
        came = None
        for k in range(1, self.ns):
            total = parts[k] if came is None else parts[k].astype(F32) + came.astype(F32)
            came = self.step_s(gate(k, total.astype(BF)))
        return parts[0], came

    def scatter_f(self, part, gate=lambda k, value, sent: value):
        came, sent = None, []
        for k in range(1, self.nz + 1):
            mine, away = part(k % self.nz, sent)
            other = self.swap_c(away)
            if k == self.nz:
                return (mine, other, came), sent
            total = mine.astype(F32) + other.astype(F32)
            if came is not None:
                total = total + came.astype(F32)
            sent.append(gate(k, total.astype(BF), sent))
            came = self.step_z(sent[-1])


def split(values, count):
    return tuple(values[:count]), list(values[count:])


def total_of(terms):
    return sum(term.astype(F32) for term in terms)


def pack_ffn_kernel(fcols, gate_ref, up_ref, out_ref):
    for i in range(gate_ref.shape[1] // fcols):
        for t in range(fcols // FTILE):
            here = slice(i * fcols + t * FTILE, i * fcols + (t + 1) * FTILE)
            out_ref[i, :, 2 * t * FTILE : (2 * t + 1) * FTILE] = gate_ref[:, here]
            out_ref[i, :, (2 * t + 1) * FTILE : (2 * t + 2) * FTILE] = up_ref[:, here]


def pack_ffn(w_gate, w_up, nf):
    own, hidden = w_gate.shape
    fcols = hidden // nf
    return pl.pallas_call(
        functools.partial(pack_ffn_kernel, fcols),
        grid=(nf // 2,),
        in_specs=[pl.BlockSpec((own, 2 * fcols), lambda i: (0, i))] * 2,
        out_specs=pl.BlockSpec((2, own, 2 * fcols), lambda i: (i, 0, 0)),
        out_shape=shape_of(nf, own, 2 * fcols),
    )(w_gate, w_up)


def unpack_ffn_kernel(fcols, w_gate_ref, w_up_ref, gain_ref, in_ref, *out_refs):
    gate_ref, up_ref, gain_out_ref = out_refs
    total = jnp.zeros(gain_out_ref.shape, F32)
    for t in range(fcols // FTILE):
        here = slice(t * FTILE, (t + 1) * FTILE)
        gate = in_ref[0, :, 2 * t * FTILE : (2 * t + 1) * FTILE].astype(F32)
        upward = in_ref[0, :, (2 * t + 1) * FTILE : (2 * t + 2) * FTILE].astype(F32)
        gate_ref[:, here] = gate
        up_ref[:, here] = upward
        both = gate * w_gate_ref[:, here].astype(F32) + upward * w_up_ref[:, here].astype(F32)
        total = total + jnp.sum(both, axis=1, keepdims=True)

    @pl.when(pl.program_id(0) == 0)
    def _():
        gain_out_ref[...] = jnp.zeros_like(gain_out_ref)

    gain_out_ref[...] += total / gain_ref[...]


def unpack_ffn(w_gate, w_up, gain, blocks):
    own, hidden = w_gate.shape
    nf = blocks.shape[0]
    fcols = hidden // nf
    wide = pl.BlockSpec((own, fcols), lambda i: (0, i))
    thin = pl.BlockSpec((own, 1), lambda i: (0, 0))
    gate, upward, grad_gain = pl.pallas_call(
        functools.partial(unpack_ffn_kernel, fcols),
        grid=(nf,),
        in_specs=[wide, wide, thin, pl.BlockSpec((1, own, 2 * fcols), lambda i: (i, 0, 0))],
        out_specs=[wide, wide, thin],
        out_shape=[
            shape_of(own, hidden, dtype=F32),
            shape_of(own, hidden, dtype=F32),
            shape_of(own, 1, dtype=F32),
        ],
    )(w_gate, w_up, gain, blocks)
    return gate, upward, grad_gain[:, 0]


def head_of(s, j, ns, nf, per_head):
    sh, fl = divmod(s, per_head)
    return (j * per_head + fl) * (ns // per_head) + sh


def pack_heads_kernel(ns, nf, per_head, *refs):
    *in_refs, extra_ref, out_ref = refs
    heads = HEADS // ns
    own = in_refs[0].shape[0]
    for s in range(ns):
        out_ref[s, own:, :] = jnp.zeros((EXTRA, out_ref.shape[2]), BF)
        out_ref[s, own:, : extra_ref.shape[1]] = extra_ref[...]
        for i, ref in enumerate(in_refs):
            for j in range(heads):
                h = head_of(s, j, ns, nf, per_head)
                at = (i * heads + j) * HEAD_DIM
                out_ref[s, :own, at : at + HEAD_DIM] = ref[:, h * HEAD_DIM : (h + 1) * HEAD_DIM]


def pack_heads(weights, extra, ns, nf, per_head):
    own, width = weights[0].shape
    return pl.pallas_call(
        functools.partial(pack_heads_kernel, ns, nf, per_head),
        in_specs=[WHOLE] * 4,
        out_specs=WHOLE,
        out_shape=shape_of(ns, own + EXTRA, 3 * width // ns),
        compiler_params=PARAMS,
    )(*weights, extra)


def unpack_heads_kernel(ns, nf, per_head, in_ref, gain_ref, *refs):
    weight_refs, grad_refs, gain_out_ref = refs[:3], refs[3:6], refs[6]
    heads = HEADS // ns
    total = jnp.zeros(gain_out_ref.shape, F32)
    for s in range(ns):
        for i in range(3):
            for j in range(heads):
                h = head_of(s, j, ns, nf, per_head)
                at = (i * heads + j) * HEAD_DIM
                here = slice(h * HEAD_DIM, (h + 1) * HEAD_DIM)
                grad = in_ref[s, :, at : at + HEAD_DIM].astype(F32)
                grad_refs[i][:, here] = grad
                total = total + jnp.sum(
                    grad * weight_refs[i][:, here].astype(F32), axis=1, keepdims=True
                )
    gain_out_ref[...] = total / gain_ref[...]


def unpack_heads(blocks, gain, weights, ns, nf, per_head):
    own, width = weights[0].shape
    *grads, grad_gain = pl.pallas_call(
        functools.partial(unpack_heads_kernel, ns, nf, per_head),
        in_specs=[WHOLE] * 5,
        out_specs=[WHOLE] * 4,
        out_shape=[shape_of(own, width, dtype=F32)] * 3 + [shape_of(own, 1, dtype=F32)],
        compiler_params=PARAMS,
    )(blocks, gain, *weights)
    return *grads, grad_gain[:, 0]


def spin(field, cosine, sine):
    return field * cosine + pltpu.roll(field, HEAD_DIM // 2, 1) * sine


def lay_out_weight(origin_ref, blocks, start, own, ns, out_ref):
    piece = out_ref.shape[1] // ns
    for j, block in enumerate(blocks):
        row = pl.multiple_of(origin_ref[j] * own, own)
        for q in range(ns):
            out_ref[pl.ds(row, own), q * piece : (q + 1) * piece] = block[
                q * own : (q + 1) * own, start:
            ]


def weights_of(scores, scale, bias, mask):
    return jnp.where(mask, jax.nn.sigmoid(scores * scale + bias), 0.0)


def mask_of(col_ref, row_ref):
    return (row_ref[0:1, :] <= col_ref[:, 0:1]) & (row_ref[1:2, :] == col_ref[:, 1:2])


def attend_kernel(
    dims, origin_ref, input_ref, inverse_ref, cos_ref, sin_ref, col_ref, row_ref, *refs
):
    ns, nf, own, cols, scale, bias = dims
    blocks = refs[:nf]
    q_ref, k_ref, v_ref, mixed_ref, att_ref, normed_ref, gains_ref, out_w = refs[nf:]
    deep = ns * own
    lay_out_weight(origin_ref, blocks, 3 * cols, own, ns, out_w)
    for j, block in enumerate(blocks):
        here = pl.ds(pl.multiple_of(origin_ref[j] * deep, deep), deep)
        gains = block[deep : deep + EXTRA, :deep].astype(F32)
        gains_ref[:, here] = gains
        unit = input_ref[:, here].astype(F32) * inverse_ref[...]
        normed_ref[:, here] = (unit * gains[0:1, :]).astype(BF)
    for part, ref in enumerate((q_ref, k_ref, v_ref)):

        @pl.loop(0, cols // TILE)
        def _(t, part=part, ref=ref):
            at = pl.multiple_of(part * cols + t * TILE, TILE)
            total = None
            for j, block in enumerate(blocks):
                from_col = pl.multiple_of(origin_ref[j] * deep, deep)
                term = nn(normed_ref[:, pl.ds(from_col, deep)], block[:deep, pl.ds(at, TILE)])
                total = term if total is None else total + term
            for i in range(TILE // HEAD_DIM):
                field = total[:, i * HEAD_DIM : (i + 1) * HEAD_DIM]
                if part < 2:
                    field = spin(field, cos_ref[...], sin_ref[...])
                to = pl.multiple_of(t * TILE + i * HEAD_DIM, HEAD_DIM)
                ref[:, pl.ds(to, HEAD_DIM)] = field.astype(BF)

    mask = mask_of(col_ref, row_ref)

    @pl.loop(0, cols // HEAD_DIM)
    def _(h):
        here = pl.ds(pl.multiple_of(h * HEAD_DIM, HEAD_DIM), HEAD_DIM)
        weights = weights_of(nt(q_ref[:, here], k_ref[:, here]), scale, bias, mask)
        mixed_ref[:, here] = nn(weights.astype(BF), v_ref[:, here]).astype(BF)

    wide = 512

    @pl.loop(0, att_ref.shape[1] // wide)
    def _(t):
        here = pl.ds(pl.multiple_of(t * wide, wide), wide)
        att_ref[:, here] = nn(mixed_ref[...], out_w[:, here]).astype(BF)


def attend(dims, origin, rows, inverse, tables, marks, blocks):
    ns, nf, own, cols, _, _ = dims
    group, width = rows.shape
    small = shape_of(group, cols)
    return pl.pallas_call(
        functools.partial(attend_kernel, dims),
        in_specs=[pl.BlockSpec(memory_space=pltpu.SMEM)] + [WHOLE] * (6 + nf),
        out_specs=[WHOLE] * 7,
        out_shape=[small] * 4
        + [shape_of(group, width)] * 2
        + [shape_of(EXTRA, width, dtype=F32)],
        scratch_shapes=[pltpu.VMEM((cols, width), BF)],
        compiler_params=PARAMS,
        cost_estimate=cost(
            2 * group * width * cols * 4 + 4 * group * group * cols, 2 * width * cols * 4
        ),
    )(origin, rows, inverse, *tables, *marks, *blocks)


def attend_back_kernel(
    dims, origin_ref, datt_ref, q_ref, k_ref, v_ref, mixed_ref, cos_ref, sin_ref, col_ref, row_ref,
    *refs
):
    ns, nf, own, cols, scale, bias = dims
    blocks = refs[:nf]
    d_qkv, out_term, out_w = refs[nf:]
    piece = datt_ref.shape[1] // ns
    lay_out_weight(origin_ref, blocks, 0, own, ns, out_w)
    mask = mask_of(col_ref, row_ref)

    @pl.loop(0, cols // HEAD_DIM)
    def _(h):
        start = pl.multiple_of(h * HEAD_DIM, HEAD_DIM)
        here = pl.ds(start, HEAD_DIM)
        query, key = q_ref[:, here], k_ref[:, here]
        d_mixed = nt(datt_ref[...], out_w[here, :]).astype(BF)
        weights = weights_of(nt(query, key), scale, bias, mask)
        d_weights = nt(d_mixed, v_ref[:, here])
        d_scores = (d_weights * weights * (1.0 - weights)).astype(BF)
        d_query = nn(d_scores, key) * scale
        d_key = tn(d_scores, query) * scale
        d_value = tn(weights.astype(BF), d_mixed)
        d_qkv[:, here] = spin(d_query, cos_ref[...], -sin_ref[...]).astype(BF)
        d_qkv[:, pl.ds(pl.multiple_of(cols + start, HEAD_DIM), HEAD_DIM)] = spin(
            d_key, cos_ref[...], -sin_ref[...]
        ).astype(BF)
        d_qkv[:, pl.ds(pl.multiple_of(2 * cols + start, HEAD_DIM), HEAD_DIM)] = d_value.astype(BF)

    @pl.loop(0, ns)
    def _(q):
        here = pl.ds(pl.multiple_of(q * piece, piece), piece)
        out_term[q] = tn(mixed_ref[...], datt_ref[:, here]).astype(BF)


def attend_back(dims, origin, datt, saved, tables, marks, blocks):
    ns, nf, own, cols, _, _ = dims
    group, width = datt.shape
    piece = width // ns
    last = pl.BlockSpec((ns * own, piece), lambda i: (0, 3 * cols // piece))

    def full(*shape):
        return pl.BlockSpec(shape, lambda i: (0,) * len(shape))

    arrays = [datt, *saved, *tables, *marks]
    return pl.pallas_call(
        functools.partial(attend_back_kernel, dims),
        grid=(1,),
        in_specs=[pl.BlockSpec(memory_space=pltpu.SMEM)]
        + [full(*array.shape) for array in arrays]
        + [last] * nf,
        out_specs=[full(group, 3 * cols), full(ns, cols, piece)],
        out_shape=[shape_of(group, 3 * cols), shape_of(ns, cols, piece)],
        scratch_shapes=[pltpu.VMEM((cols, width), BF)],
        compiler_params=PARAMS,
        cost_estimate=cost(
            2 * group * width * cols * 2 + 10 * group * group * cols, 4 * width * cols
        ),
    )(origin, *arrays, *blocks)


def weight_grad_kernel(dims, step, origin_ref, normed_ref, d_ref, out_ref, mine_ref, away_ref):
    ns, nf, own, cols, _, _ = dims
    deep = ns * own
    for i, ref in enumerate((mine_ref, away_ref)):
        origin = origin_ref[2 * step + i]
        here = pl.ds(pl.multiple_of(origin * deep, deep), deep)
        ref[:, : 3 * cols] = tn(normed_ref[:, here], d_ref[...]).astype(BF)
        row = pl.multiple_of(origin * own, own)
        for q in range(ns):
            ref[q * own : (q + 1) * own, 3 * cols :] = out_ref[q, pl.ds(row, own), :]


def weight_grad(dims, step, origin, normed, d_qkv, out_term):
    ns, nf, own, cols, _, _ = dims
    term = shape_of(ns * own, 3 * cols + out_term.shape[2])
    return pl.pallas_call(
        functools.partial(weight_grad_kernel, dims, step),
        in_specs=[pl.BlockSpec(memory_space=pltpu.SMEM)] + [WHOLE] * 3,
        out_specs=[WHOLE] * 2,
        out_shape=[term, term],
        compiler_params=PARAMS,
        cost_estimate=cost(12 * normed.shape[0] * ns * own * cols, 2**23),
    )(origin, normed, d_qkv, out_term)


def input_grad_kernel(dims, origin_ref, d_ref, *refs):
    ns, nf, own, cols, _, _ = dims
    *blocks, dn_ref = refs
    deep = ns * own
    for j, block in enumerate(blocks):
        here = pl.ds(pl.multiple_of(origin_ref[j] * deep, deep), deep)
        dn_ref[:, here] = nt(d_ref[...], block[:deep, : 3 * cols]).astype(BF)


def input_grad(dims, origin, d_qkv, blocks, width):
    ns, nf, own, cols, _, _ = dims
    group = d_qkv.shape[0]
    return pl.pallas_call(
        functools.partial(input_grad_kernel, dims),
        in_specs=[pl.BlockSpec(memory_space=pltpu.SMEM)] + [WHOLE] * (1 + nf),
        out_specs=WHOLE,
        out_shape=shape_of(group, width),
        compiler_params=PARAMS,
        cost_estimate=cost(6 * group * width * cols, 8 * width * cols),
    )(origin, d_qkv, *blocks)


def ffn_kernel(count, first, *refs):
    unit_refs, cot_refs, refs = refs[:count], refs[count : 2 * count], refs[2 * count :]
    weight_ref, down_ref = refs[:2]
    refs = refs[2 if first else 6 :]
    inner_ref, d_ref, unit_ref, cot_ref = refs[:4]
    two_refs, out_refs, two, out = refs[4 : 4 + count], refs[4 + count : 4 + 2 * count], *refs[-2:]
    rows = unit_refs[0].shape[0]
    j = pl.program_id(0)

    @pl.when(j == 0)
    def _():
        for i in range(count):
            unit_ref[i * rows : (i + 1) * rows, :] = unit_refs[i][...]
            cot_ref[i * rows : (i + 1) * rows, :] = cot_refs[i][...]

    both = nn(unit_ref[...], weight_ref[...])
    d_inner = nt(cot_ref[...], down_ref[...])
    gate, upward = both[:, :FTILE], both[:, FTILE:]
    sigma = jax.nn.sigmoid(gate)
    silu = gate * sigma
    inner_ref[...] = (silu * upward).astype(BF)
    d_ref[:, :FTILE] = (d_inner * upward * sigma * (1.0 + gate * (1.0 - sigma))).astype(BF)
    d_ref[:, FTILE:] = (d_inner * silu).astype(BF)
    two_term = nt(d_ref[...], weight_ref[...])
    out_term = nn(inner_ref[...], down_ref[...])

    @pl.when(j == 0)
    def _():
        two[...] = two_term
        out[...] = out_term

    @pl.when(j > 0)
    def _():
        two[...] += two_term
        out[...] += out_term

    @pl.when(j == pl.num_programs(0) - 1)
    def _():
        for i in range(count):
            two_refs[i][...] = two[i * rows : (i + 1) * rows, :].astype(BF)
            out_refs[i][...] = out[i * rows : (i + 1) * rows, :].astype(BF)


def ffn(turn, turns, units, cots, weight, down, before):
    rows, width = units[0].shape
    count = len(units)
    fcols = down.shape[0]
    all_rows = count * rows
    whole = pl.BlockSpec((rows, width), lambda j: (0, 0))
    shared = [
        ((all_rows, FTILE), lambda j: (turn, j), fcols),
        ((all_rows, 2 * FTILE), lambda j: (turn, j), 2 * fcols),
        ((all_rows, width), lambda j: (turn, 0), width),
        ((all_rows, width), lambda j: (turn, 0), width),
    ]
    return pl.pallas_call(
        functools.partial(ffn_kernel, count, not before),
        grid=(fcols // FTILE,),
        in_specs=[whole] * (2 * count)
        + [
            pl.BlockSpec((width, 2 * FTILE), lambda j: (0, j)),
            pl.BlockSpec((FTILE, width), lambda j: (j, 0)),
        ]
        + [pl.BlockSpec(memory_space=pl.ANY)] * len(before),
        out_specs=[pl.BlockSpec(shape, at) for shape, at, _ in shared] + [whole] * (2 * count),
        out_shape=[shape_of(turns * all_rows, last) for _, _, last in shared]
        + [shape_of(rows, width)] * (2 * count),
        scratch_shapes=[pltpu.VMEM((all_rows, width), F32)] * 2,
        input_output_aliases={2 * count + 2 + i: i for i in range(len(before))},
        compiler_params=FFN_PARAMS,
        cost_estimate=cost(
            12 * all_rows * width * fcols, 2 * (3 * fcols + 4 * all_rows) * width
        ),
    )(*units, *cots, weight, down, *before)


def norm_two_kernel(ns, nf, own, input_ref, part_ref, came_ref, gain_ref, *out_refs):
    residual_ref, inverse_ref, unit_ref = out_refs
    residual = (
        input_ref[...].astype(F32) + part_ref[...].astype(F32) + came_ref[...].astype(F32)
    )
    inverse = lax.rsqrt(jnp.mean(residual * residual, axis=-1, keepdims=True) + EPSILON)
    residual_ref[...] = residual
    inverse_ref[...] = inverse
    normed = (residual * inverse * gain_ref[...]).astype(BF)
    for f in range(nf):
        for s in range(ns):
            here, there = (f * ns + s) * own, (s * nf + f) * own
            unit_ref[:, there : there + own] = normed[:, here : here + own]


def norm_two(ns, nf, own, rows, part, came, gain):
    count, width = rows.shape
    return pl.pallas_call(
        functools.partial(norm_two_kernel, ns, nf, own),
        in_specs=[WHOLE] * 4,
        out_specs=[WHOLE] * 3,
        out_shape=[
            shape_of(count, width, dtype=F32),
            shape_of(count, 1, dtype=F32),
            shape_of(count, width),
        ],
        compiler_params=PARAMS,
    )(rows, part, came, gain)


def norm_two_back_kernel(ns, nf, own, *refs):
    term_refs, (residual_ref, inverse_ref, gain_ref, cot_ref) = refs[:3], refs[3:7]
    d_ref, low_ref, scaled = refs[7:]
    total = term_refs[0][...].astype(F32)
    for ref in term_refs[1:]:
        total = total + ref[...].astype(F32)
    for f in range(nf):
        for s in range(ns):
            here, there = (f * ns + s) * own, (s * nf + f) * own
            scaled[:, here : here + own] = total[:, there : there + own]
    unit = residual_ref[...] * inverse_ref[...]
    back = scaled[...] * gain_ref[...]
    mean = jnp.mean(back * unit, axis=-1, keepdims=True)
    d_residual = cot_ref[...].astype(F32) + inverse_ref[...] * (back - unit * mean)
    d_ref[...] = d_residual
    low_ref[...] = d_residual.astype(BF)


def norm_two_back(ns, nf, own, terms, residual, inverse, gain, cot):
    count, width = residual.shape
    return pl.pallas_call(
        functools.partial(norm_two_back_kernel, ns, nf, own),
        in_specs=[WHOLE] * 7,
        out_specs=[WHOLE] * 2,
        out_shape=[shape_of(count, width, dtype=F32), shape_of(count, width)],
        scratch_shapes=[pltpu.VMEM((count, width), F32)],
        compiler_params=PARAMS,
    )(*terms, residual, inverse, gain, cot)


def shards(
    inputs,
    positions,
    seq_ids,
    attn_gain,
    w_query,
    w_key,
    w_value,
    w_out,
    ffn_gain,
    w_gate,
    w_up,
    w_down,
    cotangent,
):
    net = Net()
    ns, nf, nz = net.ns, net.nf, net.nz
    rows, width = inputs.shape
    group = rows * ns
    own = w_query.shape[0]
    hidden = w_gate.shape[1]
    fcols = hidden // nf
    per_head = HEAD_DIM // own
    swap_head = []
    for f in range(nf):
        for s in range(ns):
            fh, fl = divmod(f, per_head)
            sh, sl = divmod(s, per_head)
            swap_head.append((s * nf + f, (sh * per_head + fl) * nf + fh * per_head + sl))
    cols = HEADS // ns * HEAD_DIM
    piece = width // ns
    dims = (ns, nf, own, cols, HEAD_DIM ** (-0.5), -math.log(group))

    origin = net.origin_f()
    extra = jnp.stack(
        [
            (positions // 256).astype(BF),
            (positions % 256).astype(BF),
            seq_ids.astype(BF),
            jnp.pad(jnp.concatenate([attn_gain, ffn_gain]), (0, rows - 2 * own)),
        ]
    )
    extra = jnp.pad(extra, ((0, EXTRA - 4), (0, 0)))

    down_all = lax.all_gather(w_down, "seq", axis=0, tiled=True)
    packed_ffn = pack_ffn(w_gate, w_up, nf)
    ffn_rows = lax.all_to_all(packed_ffn, "fsdp", split_axis=0, concat_axis=0, tiled=True)
    packed = pack_heads((w_query, w_key, after(w_value, packed_ffn)), extra, ns, nf, per_head)
    qkv_rows = net.swap_s(packed)
    out_rows = lax.ppermute(w_out, BOTH, swap_head)
    input_ring = net.ring_s(inputs)
    marks = qkv_rows[:, own : own + 4, :rows].astype(F32)
    gain_rows = marks[:, 3, : 2 * own].reshape(ns, 2, own).transpose(1, 0, 2).reshape(2, ns * own)
    merged = jnp.concatenate(
        [
            qkv_rows[:, :own].reshape(ns * own, 3 * cols),
            out_rows.reshape(own, ns, piece).transpose(1, 0, 2).reshape(ns * own, piece),
        ],
        axis=1,
    )
    merged = jnp.concatenate(
        [
            merged,
            jnp.pad(gain_rows.astype(BF), ((0, EXTRA - 2), (0, 3 * cols + piece - ns * own))),
        ],
        axis=0,
    )
    blocks = net.ring_f(merged)
    w_ffn = lax.all_gather(
        after(ffn_rows, blocks[2]).reshape(nf * own, 2 * fcols), "seq", axis=0, tiled=True
    )

    input_all = jnp.concatenate(input_ring, axis=0)
    squares = jnp.mean(jnp.square(input_all.astype(F32)), axis=-1, keepdims=True)
    inverse_all = lax.rsqrt(squares + EPSILON)
    input_float = inputs.astype(F32)
    inverse_one = inverse_all[:rows]
    unit_one = input_float * inverse_one
    order = [net.s_back(k) for k in range(ns)]
    marks = jnp.stack([lax.dynamic_index_in_dim(marks, s, 0, keepdims=False) for s in order])
    places = (marks[:, 0] * 256.0 + marks[:, 1]).reshape(group)
    ids = marks[:, 2].reshape(group)
    index = jnp.concatenate([(s * rows + jnp.arange(rows)).astype(F32) for s in order])
    frequency = 10000.0 ** (-(jnp.arange(HEAD_DIM // 2, dtype=F32) * 2.0) / HEAD_DIM)
    angles = places[:, None] * frequency[None, :]
    cosine, sine = jnp.cos(angles), jnp.sin(angles)
    tables = (
        jnp.concatenate([cosine, cosine], axis=1),
        jnp.concatenate([-sine, sine], axis=1),
    )
    row_marks = jnp.stack([index, ids])
    pair_marks = (row_marks.T, row_marks)

    *saved, attended, normed_all, gains = attend(
        dims, origin, input_all, inverse_all, tables, pair_marks, blocks
    )
    gain_one, gain_two = gains[0:1], gains[1:2]
    cots = net.ring_f(after(cotangent, blocks[-2]))
    att_terms = net.scatter_s(
        attended.reshape(ns, rows, width),
        lambda k, value: after(value, cots[2 * k]) if k < nz else value,
    )

    residual, inverse_two, unit_low = norm_two(ns, nf, own, inputs, *att_terms, gain_two)
    unit_two = residual * inverse_two
    turns = 2 if nz % 2 == 0 else 1
    each = 2 * nz // turns
    shared, two_parts, out_parts = (), [], []
    units = []

    def run_turn(turn, ready):
        nonlocal shared
        here = slice(each * turn, each * (turn + 1))
        shared, done = split(
            ffn(turn, turns, units_at(here, ready), cots[here], w_ffn, down_all, shared), 4
        )
        two_parts.extend(done[:each])
        out_parts.extend(done[each:])

    def units_at(here, ready):
        return units[here] if ready is None else after(units[here], ready)

    held_unit = unit_low
    for k in range(nz):
        if k:
            held_unit = net.step_z(
                after(held_unit, two_parts[0]) if k == each // 2 + 1 else held_unit
            )
        units += [held_unit, net.swap_c(held_unit)]
        if 2 * k + 2 == each:
            run_turn(0, None)
    sums = {}

    def two_part(k, sent):
        if 2 * k + 2 > len(two_parts):
            run_turn(1, sent[0])
        return two_parts[2 * k : 2 * k + 2]

    def two_gate(k, value, sent):
        if k == nz - 1:
            inner, d_ffn, unit_all, cot_all = shared
            sums["down"] = tn(after(inner, sent[-1]), cot_all).astype(BF)
            return after(value, sums["down"])
        return value

    two_terms, two_sent = net.scatter_f(two_part, two_gate)
    inner, d_ffn, unit_all, cot_all = shared
    grad_down = lax.psum_scatter(
        sums["down"], "seq", scatter_dimension=0, tiled=True
    ).astype(F32)
    sums["ffn"] = tn(after(unit_all, two_sent[-1]), d_ffn).astype(BF)
    two_terms = (after(two_terms[0], sums["ffn"]), *two_terms[1:])
    d_residual, d_low = norm_two_back(
        ns, nf, own, two_terms, residual, inverse_two, gain_two, cotangent
    )
    d_attended, out_came = [d_low], [None]

    def send_out(k, ready):
        other = net.swap_c(out_parts[2 * k + 1])
        total = out_parts[2 * k].astype(F32) + other.astype(F32)
        if k > 1:
            total = total + out_came[-1].astype(F32)
        out_came.append(net.step_z(after(total.astype(BF), ready)))

    for k in range(1, ns):
        value = d_attended[-1]
        d_attended.append(net.step_s(after(value, out_came[1]) if k == ns - 1 else value))
        if k == 1:
            send_out(1, d_attended[1])
    ffn_sum = lax.psum_scatter(
        after(sums["ffn"], d_attended[-1]).reshape(ns, nf * own, 2 * fcols),
        "seq",
        scatter_dimension=0,
        tiled=False,
    )
    for k in range(2, nz):
        send_out(k, d_low)
    out_terms = (out_parts[0], net.swap_c(out_parts[1]), out_came[-1])
    layer_out = (residual + total_of(out_terms)).astype(BF)
    d_qkv, out_grad = attend_back(
        dims, origin, jnp.concatenate(d_attended, axis=0), saved, tables, pair_marks, blocks
    )
    held = {}

    def weight_part(k, sent):
        if k == 1:
            ready = after(d_qkv, out_came[-2])
        else:
            ready = after(d_qkv, sent[min(len(sent), 2) - 1])
        return weight_grad(dims, k, origin, normed_all, ready, out_grad)

    def weight_gate(k, value, sent):
        if k == 2:
            dn_parts = input_grad(dims, origin, after(d_qkv, sent[0]), blocks, width)
            held["one"] = total_of(net.scatter_s(dn_parts.reshape(ns, rows, width)))
            return after(value, out_terms[2])
        return value

    terms, weight_sent = net.scatter_f(weight_part, weight_gate)
    ffn_own = lax.all_to_all(
        after(ffn_sum, weight_sent[-1]).reshape(nf, own, 2 * fcols), "fsdp", split_axis=0, concat_axis=0, tiled=True
    )
    grad_gate, grad_up, grad_ffn_gain = unpack_ffn(
        w_gate,
        w_up,
        ffn_gain.astype(F32)[:, None],
        ffn_own,
    )
    one_sum = held["one"]
    scaled_one = one_sum * gain_one
    grad_input = d_residual + inverse_one * (
        scaled_one - unit_one * jnp.mean(scaled_one * unit_one, axis=-1, keepdims=True)
    )
    term = total_of(terms).astype(BF)
    qkv_own = net.swap_s(term[:, : 3 * cols].reshape(ns, own, 3 * cols))
    grad_query, grad_key, grad_value, grad_attn_gain = unpack_heads(
        qkv_own, attn_gain.astype(F32)[:, None], (w_query, w_key, w_value), ns, nf, per_head
    )
    out_mine = term[:, 3 * cols :].reshape(ns, own, piece).transpose(1, 0, 2).reshape(own, width)
    back_head = [(b, a) for a, b in swap_head]
    grad_out = lax.ppermute(out_mine, BOTH, back_head).astype(F32)
    return (
        layer_out,
        grad_input,
        grad_attn_gain,
        grad_query,
        grad_key,
        grad_value,
        grad_out,
        grad_ffn_gain,
        grad_gate,
        grad_up,
        grad_down,
    )


def solution(mesh):
    row = P(("fsdp", "seq"), None)
    flat = P(("fsdp", "seq"))
    return jax.shard_map(
        shards,
        mesh=mesh,
        in_specs=(row, flat, flat, flat, row, row, row, row, flat, row, row, row, row),
        out_specs=(row, row, flat, row, row, row, row, flat, row, row, row),
        check_vma=False,
    )
```
